768 devices in a mesh: sub: 48 (over z, x_hi, core), blk: 16 (over x_lo, y).
Axes of the slice: x: 4 (x_hi: 2, x_lo: 2; x = x_hi * 2 + x_lo), y: 8, z: 12, core: 2. Of those that a mesh axis runs over, the one named last changes fastest.
Arguments:
- stiffness: bfloat16 [48, 2048, 128, 128], P('sub', 'blk')
- dofmap: int32 [48, 2048, 128], P('sub', 'blk'), may hold values from 0 to 16383
- eigvecs: bfloat16 [48, 64, 16384], P('sub', None, 'blk'), may hold values from -6 to 6
- rim_rows: int32 [48, 2, 2048], P('sub'), may hold values from 0 to 16383
- owner_map: int32 [48], replicated, may hold values from 0 to 47, as said below
Outputs:
- coarse_rows: float32 [192, 64, 192], P('sub', 'blk')
The draws below stay inside these ranges and needn't reach their ends.
Inputs may be any that keep to these rules, and one draw needn't show every extreme that they name: `owner_map`: each solver index names at most 4 subdomains, and one names exactly 4.
All inputs are finite; a program needn't handle non-finite values.
Results may differ from the reference program's by a relative error of at most 0.0003.
Values may be sent and summed in bfloat16 or wider, within the bound.
No kernel may reach another device: no remote copies, remote signals or barrier semaphores. Data moves between devices by JAX's collectives and lax.ppermute only.
A program may use at most 64 MiB of HBM per device.

```python
import math
import jax
import jax.numpy as jnp
from jax import lax

K = 64
EB = 128
CAP = 4
OV = 2048
NL = 16384
EBLK = 2048
N_SUB = 48


def draw_stiffness(key, part):
    entries = jax.random.normal(jax.random.fold_in(key, 11), (N_SUB, EBLK, EB, EB), jnp.float32)
    entries = entries * EB ** (-0.5)
    symmetric = (entries + jnp.swapaxes(entries, 2, 3)) * 0.7071
    return symmetric.astype(jnp.bfloat16)


def draw_owner_map(key, part):
    base = jax.random.fold_in(key, 23)
    key_shift, key_order = jax.random.split(base, 2)
    shift = jax.random.randint(key_shift, (), 0, N_SUB).astype(jnp.int32)
    half = N_SUB // 2
    tail_count = N_SUB - CAP - 2
    position = jnp.arange(N_SUB, dtype=jnp.int32)
    relative = (position - shift) % N_SUB
    order = jax.random.permutation(key_order, tail_count).astype(jnp.int32)
    tail_pick = jnp.take(order, jnp.clip(relative - CAP - 2, 0, tail_count - 1))
    tail_owner = shift + half + CAP + 2 + tail_pick
    busiest = shift + half + 1
    owner = jnp.where(relative == 0, position + half, jnp.where(relative == 1, position + 1, jnp.where(relative <= CAP + 1, busiest, tail_owner)))
    owner = owner % N_SUB
    turned = (owner + (N_SUB - 1) - owner[0]) % N_SUB
    return turned.astype(jnp.int32)


def plant(values, stream_key, least, largest):
    longest = values.shape.index(max(values.shape))
    spots = []
    for shift in (0, 1):
        where = [jax.random.randint(jax.random.fold_in(stream_key, axis), (), 0, length) for axis, length in enumerate(values.shape)]
        where[longest] = (where[longest] + shift) % values.shape[longest]
        spots.append(tuple(where))
    return values.at[spots[0]].set(least).at[spots[1]].set(largest)


def block_scale(rng, shape, cuts, smallest, high):
    level, own = 1.0, jax.random.fold_in(rng, 6)
    for axis_at, blocks in cuts:
        draws = jnp.exp(jax.random.uniform(jax.random.fold_in(own, axis_at), (blocks,), jnp.float32, smallest / len(cuts), high / len(cuts)))
        level = level * jnp.repeat(draws, shape[axis_at] // blocks).reshape([-1 if axis == axis_at else 1 for axis in range(len(shape))])
    return level


def noise(own_key, extent, width, most, shards=(), kind=jnp.bfloat16):
    loudness = block_scale(own_key, extent, shards, -0.22, 0.18) if shards else 1.0
    result = jax.random.normal(own_key, extent, jnp.float32) * width * loudness
    return jnp.minimum(jnp.maximum(result, -most), most).astype(kind)


def setup_inputs(seed: int = 0) -> dict:
    splits = jax.random.split(jax.random.key(seed), 6)
    return {
        "stiffness": draw_stiffness(jax.random.fold_in(splits[5], 71), 0),
        "dofmap": plant(jax.random.randint(splits[1], (N_SUB, EBLK, EB), 0, NL), jax.random.fold_in(splits[1], 1), 0, NL - 1).astype(jnp.int32),
        "eigvecs": noise(splits[2], (N_SUB, K, NL), 1.0, 6.0, ((0, 48), (2, 16))),
        "rim_rows": plant(jax.random.randint(splits[3], (N_SUB, 2, OV), 0, NL), jax.random.fold_in(splits[3], 1), 0, NL - 1).astype(jnp.int32),
        "owner_map": draw_owner_map(jax.random.fold_in(splits[5], 71), 0),
    }


def apply_blocks(operands):
    blocks, block_dofs, mode_rows = operands
    flat_dofs = block_dofs.reshape(-1)
    picked = jnp.take(mode_rows, flat_dofs, axis=1).reshape(K, EBLK, EB).astype(jnp.float32)
    products = jnp.einsum('kbe,bef->kbf', picked, blocks.astype(jnp.float32))
    return jnp.zeros((K, NL), jnp.float32).at[:, flat_dofs].add(products.reshape(K, -1))

def reference(stiffness, dofmap, eigvecs, rim_rows, owner_map):
    operator_image = lax.map(apply_blocks, (stiffness, dofmap, eigvecs))
    modes_wide = eigvecs.astype(jnp.float32)
    high = lax.Precision.HIGHEST
    diagonal_block = jnp.einsum('skn,sjn->skj', modes_wide, operator_image, precision=high)
    take_rows = jax.vmap(lambda mat, idx: jnp.take(mat, idx, axis=1))
    image_before = take_rows(operator_image, rim_rows[:, 0])
    image_after = take_rows(operator_image, rim_rows[:, 1])
    left_modes = take_rows(modes_wide, rim_rows[:, 0])
    right_modes = take_rows(modes_wide, rim_rows[:, 1])
    empty_rim = jnp.zeros((1, K, OV), jnp.float32)
    prev_right = jnp.concatenate([empty_rim, image_after[:-1]], axis=0)
    next_left = jnp.concatenate([image_before[1:], empty_rim], axis=0)
    left_block = jnp.einsum('skn,sjn->skj', left_modes, prev_right, precision=high)
    right_block = jnp.einsum('skn,sjn->skj', right_modes, next_left, precision=high)
    row_scale = 1.0 / math.sqrt(EBLK * EB)
    coarse = jnp.concatenate([left_block, diagonal_block, right_block], axis=2) * row_scale
    positions = jnp.arange(N_SUB, dtype=jnp.int32)
    same_owner = owner_map[:, None] == owner_map[None, :]
    earlier = positions[None, :] < positions[:, None]
    slot_rank = lax.optimization_barrier(jnp.sum((same_owner & earlier).astype(jnp.int32), axis=1))
    slot_index = (owner_map * CAP + slot_rank).astype(jnp.int32)
    return jnp.zeros((N_SUB * CAP, K, 3 * K), jnp.float32).at[slot_index].set(coarse)
```

```python
import functools
import math

import jax
import jax.numpy as jnp
from jax import lax
from jax.experimental import pallas as pl
from jax.experimental.pallas import tpu as pltpu
from jax.sharding import PartitionSpec as P

CAP = 4
LANES = 128
CHUNK = 128
GROUP = 16
TOGETHER = 8
F32 = jnp.float32
BF16 = jnp.bfloat16
VMEM = pl.BlockSpec(memory_space=pltpu.VMEM)
SMEM = pl.BlockSpec(memory_space=pltpu.SMEM)


def low_lanes(rows):
    return lax.broadcasted_iota(jnp.int32, (rows, LANES), 1) < LANES // 2


def pack_kernel(modes_ref, out_ref):
    wide = modes_ref[...].astype(F32)
    half = wide.shape[1] // 2
    stacked = jnp.concatenate([wide[:, :half], wide[:, half:]], axis=0)
    out_ref[...] = stacked.T.astype(BF16)


def pack(modes):
    count, width = modes.shape
    return pl.pallas_call(
        pack_kernel,
        out_shape=jax.ShapeDtypeStruct((width // 2, 2 * count), BF16),
        in_specs=[VMEM],
        out_specs=VMEM,
    )(modes)


def unpack_slices(base_ref, pieces, slice_rows, table, stride=1):
    at = 0
    for piece in pieces:
        for first in range(0, piece.shape[0], slice_rows):
            base = base_ref[at]
            at += 1

            def step(c, _):
                start = pl.multiple_of(c * CHUNK, CHUNK)
                wide = piece[pl.ds(first + start, CHUNK), :].astype(F32)
                low = low_lanes(CHUNK)
                here = pl.multiple_of(base + start, CHUNK)
                there = pl.multiple_of(base + slice_rows + start, CHUNK)
                first_half = jnp.where(low, wide, 0.0)
                second_half = jnp.where(low, pltpu.roll(wide, LANES // 2, 1), 0.0)
                if stride == 1:
                    table[pl.ds(here, CHUNK), :] = first_half
                    table[pl.ds(there, CHUNK), :] = second_half
                else:
                    for at_row, value in ((here, first_half), (there, second_half)):
                        table[pl.ds(2 * at_row, CHUNK, stride=2), :] = value
                        table[pl.ds(2 * at_row + 1, CHUNK, stride=2), :] = jnp.zeros_like(value)
                return 0

            lax.fori_loop(0, slice_rows // CHUNK, step, 0)


def rim_kernel(slice_rows, n_pieces, base_ref, rim_ref, *refs):
    pieces, (left_ref, right_ref), (table, taken) = refs[:n_pieces], refs[n_pieces:n_pieces + 2], refs[n_pieces + 2:]
    unpack_slices(base_ref, pieces, slice_rows, table)
    groups, group = rim_ref.shape[0] // 2, rim_ref.shape[1]
    count = groups * group
    for side, out in ((0, left_ref), (1, right_ref)):

        def gather(g, _):
            to = taken.at[pl.ds(pl.multiple_of(g * group, group), group)]
            for j in range(group):
                to[pl.ds(j, 1), :] = table[pl.ds(rim_ref[side * groups + g, j], 1), :]
            return 0

        lax.fori_loop(0, groups, gather, 0)
        half = count // 2
        out[...] = jnp.where(
            low_lanes(half), taken[:half, :], pltpu.roll(taken[half:, :], LANES // 2, 1)
        ).astype(BF16)


def take_rim(bases, rim, pieces, slice_rows):
    total = 2 * sum(p.shape[0] for p in pieces)
    count = rim.shape[1]
    packed = jax.ShapeDtypeStruct((count // 2, LANES), BF16)
    return pl.pallas_call(
        functools.partial(rim_kernel, slice_rows, len(pieces)),
        out_shape=(packed, packed),
        in_specs=[SMEM, SMEM] + [VMEM] * len(pieces),
        out_specs=(VMEM, VMEM),
        scratch_shapes=[pltpu.VMEM((total, LANES), F32), pltpu.VMEM((count, LANES), F32)],
        compiler_params=pltpu.CompilerParams(vmem_limit_bytes=48 * 2**20),
    )(bases, rim.reshape(-1, LANES), *pieces)


def spread_rim(packed, out, high):
    half = packed.shape[0]

    def step(c, _):
        start = pl.multiple_of(c * CHUNK, CHUNK)
        wide = packed[pl.ds(start, CHUNK), :].astype(F32)
        turned = pltpu.roll(wide, LANES // 2, 1)
        low = low_lanes(CHUNK)
        if high:
            first, second = jnp.where(low, 0.0, turned), jnp.where(low, 0.0, wide)
        else:
            first, second = jnp.where(low, wide, 0.0), jnp.where(low, turned, 0.0)
        out[pl.ds(start, CHUNK), :] = first
        out[pl.ds(half + start, CHUNK), :] = second
        return 0

    lax.fori_loop(0, half // CHUNK, step, 0)


def main_kernel(
    slice_rows, n_pieces, scale, base_ref, rim_ref, clash_ref, dof_ref, stiff_ref, from_left, from_right, *refs
):
    pieces = refs[:n_pieces]
    out_ref = refs[n_pieces]
    table, rim_a, rim_b, got, acc, acc_low = refs[n_pieces + 1:]
    unpack_slices(base_ref, pieces, slice_rows, table, 2)
    spread_rim(from_left, rim_a, True)
    spread_rim(from_right, rim_b, False)
    groups = clash_ref.shape[0]
    group = rim_ref.shape[1]

    def add_rows(g, _):
        first = pl.multiple_of(g * group, group)
        new_a, new_b = rim_a.at[pl.ds(first, group)], rim_b.at[pl.ds(first, group)]

        @pl.when(clash_ref[g] == 0)
        def _():
            at_a = [2 * rim_ref[g, j] for j in range(group)]
            at_b = [2 * rim_ref[groups + g, j] + 1 for j in range(group)]
            sum_a = [table[pl.ds(row, 1), :] + new_a[pl.ds(j, 1), :] for j, row in enumerate(at_a)]
            sum_b = [table[pl.ds(row, 1), :] + new_b[pl.ds(j, 1), :] for j, row in enumerate(at_b)]
            for j in range(group):
                table[pl.ds(at_a[j], 1), :] = sum_a[j]
                table[pl.ds(at_b[j], 1), :] = sum_b[j]

        @pl.when(clash_ref[g] != 0)
        def _():
            def one(j, _):
                table[pl.ds(2 * rim_ref[g, j], 1), :] += new_a[pl.ds(j, 1), :]
                table[pl.ds(2 * rim_ref[groups + g, j] + 1, 1), :] += new_b[pl.ds(j, 1), :]
                return 0

            lax.fori_loop(0, group, one, 0)

        return 0

    lax.fori_loop(0, groups, add_rows, 0)

    n_blocks, size = dof_ref.shape
    modes = LANES // 2

    def gather(e, _):
        to = got.at[pl.ds(pl.multiple_of(2 * e * size, 2 * size), 2 * size)]
        for j in range(size):
            row = dof_ref[e, j]
            to[pl.ds(2 * j, 2), :] = table[pl.ds(2 * row, 2), :]
        return 0

    lax.fori_loop(0, n_blocks, gather, 0)

    acc[...] = jnp.zeros_like(acc)
    acc_low[...] = jnp.zeros_like(acc_low)
    width = TOGETHER * size

    def contract(i, _):
        first = pl.multiple_of(2 * i * width, 2 * width)
        wide_a, wide_b = got[pl.ds(first, width, stride=2), :], got[pl.ds(first + 1, width, stride=2), :]
        high_a, high_b = wide_a.astype(BF16), wide_b.astype(BF16)
        low_ab = ((wide_a - high_a.astype(F32)) + (wide_b - high_b.astype(F32))).astype(BF16)
        picked = high_a.T[:modes, :]
        image = jnp.concatenate(
            [
                jnp.dot(picked[:, e * size:(e + 1) * size], stiff_ref[i * TOGETHER + e], preferred_element_type=F32)
                for e in range(TOGETHER)
            ],
            axis=1,
        )
        image_high = image.astype(BF16)
        image_low = (image - image_high.astype(F32)).astype(BF16)
        both = jnp.concatenate([image_high, image_low], axis=0)
        right = jnp.concatenate([high_a, high_b], axis=1)
        acc[...] += jnp.dot(both, right, preferred_element_type=F32)
        acc_low[...] += jnp.dot(image_high, low_ab, preferred_element_type=F32)
        return 0

    lax.fori_loop(0, n_blocks // TOGETHER, contract, 0)
    summed = acc[:modes, :] + acc[modes:, :]
    first, second = summed[:, :LANES], summed[:, LANES:]
    rest = acc_low[...]
    low = low_lanes(modes)
    first = first + jnp.where(low, 0.0, rest)
    second = second + jnp.where(low, rest, 0.0)
    first_t, second_t = (first * scale).T, (second * scale).T
    own, to_prev, to_next = first_t[:modes], first_t[modes:], second_t[:modes]
    rows = jnp.concatenate([to_next, own, to_prev], axis=1)
    share = out_ref.shape[1]
    for d in range(out_ref.shape[0]):
        out_ref[d] = rows[d * share:(d + 1) * share]


def clashes(rim):
    grouped = rim.reshape(2, -1, GROUP)
    same = grouped[:, :, :, None] == grouped[:, :, None, :]
    places = jnp.arange(GROUP)
    return jnp.any(same & (places[:, None] < places[None, :]), axis=(0, 2, 3)).astype(jnp.int32)


def contract_blocks(bases, rim, dofs, stiffness, from_left, from_right, pieces, slice_rows, parts, scale):
    total = 2 * sum(p.shape[0] for p in pieces)
    count = rim.shape[1]
    modes = LANES // 2
    n_blocks, size = dofs.shape
    wide = lambda n: pltpu.VMEM((n, LANES), F32)
    return pl.pallas_call(
        functools.partial(main_kernel, slice_rows, len(pieces), scale),
        out_shape=jax.ShapeDtypeStruct((parts, modes // parts, 3 * modes), F32),
        in_specs=[SMEM, SMEM, SMEM, SMEM, VMEM, VMEM, VMEM] + [VMEM] * len(pieces),
        out_specs=VMEM,
        scratch_shapes=[
            wide(2 * total), wide(count), wide(count), wide(2 * n_blocks * size),
            pltpu.VMEM((2 * modes, 2 * LANES), F32), pltpu.VMEM((modes, LANES), F32),
        ],
        compiler_params=pltpu.CompilerParams(vmem_limit_bytes=56 * 2**20),
    )(bases, rim.reshape(-1, GROUP), clashes(rim), dofs, stiffness, from_left, from_right, *pieces)


def ring_pieces(packed, index, count):
    ring = count // 2
    move = lambda value, dx, dy: lax.ppermute(
        value, "blk",
        [(i, ((i // ring + dx) % 2) * ring + (i % ring + dy) % ring) for i in range(count)],
    )
    x, y = index // ring, index % ring
    base = lambda flip, dy: ((jnp.remainder(x + flip, 2)) * ring + jnp.remainder(y + dy, ring))
    rows = packed.shape[0]
    both = jnp.concatenate([packed, move(packed, 1, 0)], axis=0)
    pieces, places = [both], [base(0, 0), base(1, 0)]
    up = down = both
    for k in range(1, ring // 2):
        up, down = move(up, 0, 1), move(down, 0, -1)
        pieces += [up, down]
        places += [base(0, -k), base(1, -k), base(0, k), base(1, k)]
    pieces += [move(up[:rows], 0, 1), move(down[rows:], 0, -1)]
    places += [base(0, ring // 2), base(1, ring // 2)]
    return pieces, jnp.stack(places).astype(jnp.int32)


def on_device(stiffness, dofmap, eigvecs, rim_rows, owner_map):
    blk_count, sub_count = lax.axis_size("blk"), lax.axis_size("sub")
    own_rows = eigvecs.shape[2]
    slice_rows = own_rows // 2
    block_count, block_size = dofmap.shape[1:]
    blk, sub = lax.axis_index("blk"), lax.axis_index("sub")
    with jax.named_scope("pack"):
        packed = pack(eigvecs[0])
    with jax.named_scope("gather_modes"):
        pieces, places = ring_pieces(packed, blk, blk_count)
        bases = places * own_rows
    with jax.named_scope("rim"):
        left, right = take_rim(bases, rim_rows[0], pieces, slice_rows)
        from_left = lax.ppermute(right, "sub", [(i, i + 1) for i in range(sub_count - 1)])
        from_right = lax.ppermute(left, "sub", [(i + 1, i) for i in range(sub_count - 1)])
    with jax.named_scope("contract"):
        scale = 1.0 / math.sqrt(block_count * blk_count * block_size)
        share = contract_blocks(
            bases, rim_rows[0], dofmap[0], stiffness[0], from_left, from_right, pieces, slice_rows, blk_count, scale
        )
    with jax.named_scope("sum_over_blk"):
        mine = jnp.sum(lax.all_to_all(share, "blk", 0, 0, tiled=True), axis=0)
    with jax.named_scope("relay"):
        sent = jnp.broadcast_to(mine[None], (sub_count,) + mine.shape)
        arrived = lax.all_to_all(sent, "sub", 0, 0, tiled=True)
    with jax.named_scope("slots"):
        positions = jnp.arange(sub_count, dtype=jnp.int32)
        same_owner = owner_map[:, None] == owner_map[None, :]
        earlier = positions[None, :] < positions[:, None]
        slot_rank = jnp.sum((same_owner & earlier).astype(jnp.int32), axis=1)
        slot_ids = jnp.arange(CAP, dtype=jnp.int32)
        chosen = (owner_map[None, :] == sub) & (slot_rank[None, :] == slot_ids[:, None])
        none = jnp.zeros((CAP, 1), bool)
        from_prev = jnp.concatenate([chosen[:, 1:], none], axis=1)
        from_next = jnp.concatenate([none, chosen[:, :-1]], axis=1)
        modes = LANES // 2
        parts = [
            jnp.sum(jnp.where(pick[:, :, None, None], arrived[None, :, :, p * modes:(p + 1) * modes], 0.0), axis=1)
            for p, pick in enumerate((from_prev, chosen, from_next))
        ]
        return jnp.concatenate(parts, axis=2)


def solution(mesh):
    return jax.shard_map(
        on_device,
        mesh=mesh,
        in_specs=(
            P("sub", "blk", None, None),
            P("sub", "blk", None),
            P("sub", None, "blk"),
            P("sub", None, None),
            P(),
        ),
        out_specs=P("sub", "blk", None),
        check_vma=False,
    )
```

```python
import functools
import math

import jax
import jax.numpy as jnp
from jax import lax
from jax.experimental import pallas as pl
from jax.experimental.pallas import tpu as pltpu
from jax.sharding import PartitionSpec as P

CAP = 4
LANES = 128
CHUNK = 256
GROUP = 16
TOGETHER = 8
F32 = jnp.float32
BF16 = jnp.bfloat16
VMEM = pl.BlockSpec(memory_space=pltpu.VMEM)
SMEM = pl.BlockSpec(memory_space=pltpu.SMEM)


def low_lanes(rows):
    return lax.broadcasted_iota(jnp.int32, (rows, LANES), 1) < LANES // 2


def pack_kernel(modes_ref, out_ref):
    wide = modes_ref[...].astype(F32)
    half = wide.shape[1] // 2
    stacked = jnp.concatenate([wide[:, :half], wide[:, half:]], axis=0)
    out_ref[...] = stacked.T.astype(BF16)


def pack(modes):
    count, width = modes.shape
    return pl.pallas_call(
        pack_kernel,
        out_shape=jax.ShapeDtypeStruct((width // 2, 2 * count), BF16),
        in_specs=[VMEM],
        out_specs=VMEM,
    )(modes)


def index_kernel(dof_ref, rim_ref, dof_words, rim_words, clash_ref):
    size = dof_ref.shape[1]
    dofs = dof_ref[...]
    dof_words[...] = 2 * dofs + (pltpu.roll(dofs, size // 2, 1) << 17)
    rows = rim_words.shape[0]
    sides = [
        jnp.concatenate([rim_ref[side:side + 1, r * LANES:(r + 1) * LANES] for r in range(rows)], axis=0)
        for side in range(2)
    ]
    rim_words[...] = 2 * sides[0] + (sides[1] << 17)
    place = lax.broadcasted_iota(jnp.int32, (rows, LANES), 1) % GROUP
    clash = jnp.zeros((rows, LANES), jnp.int32)
    for d in range(1, GROUP):
        for side in sides:
            clash = jnp.where((pltpu.roll(side, d, 1) == side) & (place >= d), 1, clash)
    step = 1
    while step < GROUP:
        clash = jnp.maximum(clash, pltpu.roll(clash, step, 1))
        step *= 2
    clash_ref[...] = clash


def index_words(dofs, rim):
    rows = rim.shape[1] // LANES
    word = lambda r, c: jax.ShapeDtypeStruct((r, c), jnp.int32)
    return pl.pallas_call(
        index_kernel,
        out_shape=(word(*dofs.shape), word(rows, LANES), word(rows, LANES)),
        in_specs=[VMEM, VMEM],
        out_specs=(VMEM, VMEM, VMEM),
    )(dofs, rim)


def unpack_slices(base_ref, pieces, slice_rows, table, clear):
    at = 0
    for piece in pieces:
        for first in range(0, piece.shape[0], slice_rows):
            base = base_ref[at]
            at += 1

            def step(c, _):
                start = pl.multiple_of(c * CHUNK, CHUNK)
                wide = piece[pl.ds(first + start, CHUNK), :].astype(F32)
                low = low_lanes(CHUNK)
                here = pl.multiple_of(base + start, CHUNK)
                there = pl.multiple_of(base + slice_rows + start, CHUNK)
                turned = pltpu.roll(wide, LANES // 2, 1)
                for at_row, value in ((here, wide), (there, turned)):
                    if clear:
                        value = jnp.where(low, value, 0.0)
                        table[pl.ds(2 * at_row + 1, CHUNK, stride=2), :] = jnp.zeros_like(value)
                    table[pl.ds(2 * at_row, CHUNK, stride=2), :] = value
                return 0

            lax.fori_loop(0, slice_rows // CHUNK, step, 0)


def rim_kernel(slice_rows, n_pieces, base_ref, rim_ref, *refs):
    pieces, (left_ref, right_ref), (table, taken) = refs[:n_pieces], refs[n_pieces:n_pieces + 2], refs[n_pieces + 2:]
    unpack_slices(base_ref, pieces, slice_rows, table, False)
    groups, group = rim_ref.shape
    count = groups * group

    def gather(g, _):
        first = pl.multiple_of(g * group, group)
        to_left, to_right = taken.at[pl.ds(first, group)], taken.at[pl.ds(count + first, group)]
        for j in range(group):
            word = rim_ref[g, j]
            to_left[pl.ds(j, 1), :] = table[pl.ds(word & 0xFFFF, 1), :]
            to_right[pl.ds(j, 1), :] = table[pl.ds(word >> 16, 1), :]
        return 0

    lax.fori_loop(0, groups, gather, 0)
    half = count // 2
    for at, out in ((0, left_ref), (count, right_ref)):
        first, second = taken[at:at + half, :], taken[at + half:at + count, :]
        out[...] = jnp.where(low_lanes(half), first, pltpu.roll(second, LANES // 2, 1)).astype(BF16)


def take_rim(bases, rim, pieces, slice_rows):
    total = 2 * sum(p.shape[0] for p in pieces)
    count = rim.size
    packed = jax.ShapeDtypeStruct((count // 2, LANES), BF16)
    return pl.pallas_call(
        functools.partial(rim_kernel, slice_rows, len(pieces)),
        out_shape=(packed, packed),
        in_specs=[SMEM, SMEM] + [VMEM] * len(pieces),
        out_specs=(VMEM, VMEM),
        scratch_shapes=[pltpu.VMEM((2 * total, LANES), F32), pltpu.VMEM((2 * count, LANES), F32)],
        compiler_params=pltpu.CompilerParams(vmem_limit_bytes=48 * 2**20),
    )(bases, rim, *pieces)


def spread_rim(packed, out, high):
    half = packed.shape[0]

    def step(c, _):
        start = pl.multiple_of(c * CHUNK, CHUNK)
        wide = packed[pl.ds(start, CHUNK), :].astype(F32)
        turned = pltpu.roll(wide, LANES // 2, 1)
        low = low_lanes(CHUNK)
        if high:
            first, second = jnp.where(low, 0.0, turned), jnp.where(low, 0.0, wide)
        else:
            first, second = jnp.where(low, wide, 0.0), jnp.where(low, turned, 0.0)
        out[pl.ds(start, CHUNK), :] = first
        out[pl.ds(half + start, CHUNK), :] = second
        return 0

    lax.fori_loop(0, half // CHUNK, step, 0)


def main_kernel(
    slice_rows, n_pieces, scale, base_ref, rim_ref, clash_ref, dof_ref, stiff_ref, from_left, from_right, *refs
):
    pieces = refs[:n_pieces]
    out_ref = refs[n_pieces]
    table, rim_a, rim_b, got, acc, acc_low = refs[n_pieces + 1:]
    unpack_slices(base_ref, pieces, slice_rows, table, True)
    spread_rim(from_left, rim_a, True)
    spread_rim(from_right, rim_b, False)
    rim_groups, group_rows = rim_ref.shape

    def add_rows(g, _):
        first = pl.multiple_of(g * group_rows, group_rows)
        for k in range(0, group_rows, GROUP):
            new_a, new_b = rim_a.at[pl.ds(first + k, GROUP)], rim_b.at[pl.ds(first + k, GROUP)]

            @pl.when(clash_ref[g, k + GROUP - 1] == 0)
            def _(k=k, new_a=new_a, new_b=new_b):
                words = [rim_ref[g, k + j] for j in range(GROUP)]
                at = [(word & 0xFFFF, (word >> 16) + 1) for word in words]
                sums = [
                    (table[pl.ds(a, 1), :] + new_a[pl.ds(j, 1), :], table[pl.ds(b, 1), :] + new_b[pl.ds(j, 1), :])
                    for j, (a, b) in enumerate(at)
                ]
                for (a, b), (sum_a, sum_b) in zip(at, sums):
                    table[pl.ds(a, 1), :] = sum_a
                    table[pl.ds(b, 1), :] = sum_b

            @pl.when(clash_ref[g, k + GROUP - 1] != 0)
            def _(k=k, new_a=new_a, new_b=new_b):
                def one(j, _):
                    word = rim_ref[g, k + j]
                    table[pl.ds(word & 0xFFFF, 1), :] += new_a[pl.ds(j, 1), :]
                    table[pl.ds((word >> 16) + 1, 1), :] += new_b[pl.ds(j, 1), :]
                    return 0

                lax.fori_loop(0, GROUP, one, 0)

        return 0

    lax.fori_loop(0, rim_groups, add_rows, 0)

    n_blocks, size = dof_ref.shape
    modes = LANES // 2

    def gather(e, _):
        to = got.at[pl.ds(pl.multiple_of(2 * e * size, 2 * size), 2 * size)]
        for j in range(size // 2):
            word = dof_ref[e, j]
            to[pl.ds(2 * j, 2), :] = table[pl.ds(word & 0xFFFF, 2), :]
            to[pl.ds(size + 2 * j, 2), :] = table[pl.ds(word >> 16, 2), :]
        return 0

    lax.fori_loop(0, n_blocks, gather, 0)

    acc[...] = jnp.zeros_like(acc)
    acc_low[...] = jnp.zeros_like(acc_low)
    width = TOGETHER * size

    def contract(i, _):
        first = pl.multiple_of(2 * i * width, 2 * width)
        wide_a, wide_b = got[pl.ds(first, width, stride=2), :], got[pl.ds(first + 1, width, stride=2), :]
        high_a, high_b = wide_a.astype(BF16), wide_b.astype(BF16)
        low_ab = ((wide_a - high_a.astype(F32)) + (wide_b - high_b.astype(F32))).astype(BF16)
        picked = high_a.T[:modes, :]
        image = jnp.concatenate(
            [
                jnp.dot(picked[:, e * size:(e + 1) * size], stiff_ref[i * TOGETHER + e], preferred_element_type=F32)
                for e in range(TOGETHER)
            ],
            axis=1,
        )
        image_high = image.astype(BF16)
        image_low = (image - image_high.astype(F32)).astype(BF16)
        both = jnp.concatenate([image_high, image_low], axis=0)
        right = jnp.concatenate([high_a, high_b], axis=1)
        acc[...] += jnp.dot(both, right, preferred_element_type=F32)
        acc_low[...] += jnp.dot(image_high, low_ab, preferred_element_type=F32)
        return 0

    lax.fori_loop(0, n_blocks // TOGETHER, contract, 0)
    summed = acc[:modes, :] + acc[modes:, :]
    first, second = summed[:, :LANES], summed[:, LANES:]
    rest = acc_low[...]
    low = low_lanes(modes)
    first = first + jnp.where(low, 0.0, rest)
    second = second + jnp.where(low, rest, 0.0)
    first_t, second_t = (first * scale).T, (second * scale).T
    own, to_prev, to_next = first_t[:modes], first_t[modes:], second_t[:modes]
    rows = jnp.concatenate([to_next, own, to_prev], axis=1)
    share = out_ref.shape[1]
    for d in range(out_ref.shape[0]):
        out_ref[d] = rows[d * share:(d + 1) * share]


def contract_blocks(bases, rim, clash, dofs, stiffness, from_left, from_right, pieces, slice_rows, parts, scale):
    total = 2 * sum(p.shape[0] for p in pieces)
    count = rim.size
    modes = LANES // 2
    n_blocks, size = dofs.shape
    wide = lambda n: pltpu.VMEM((n, LANES), F32)
    return pl.pallas_call(
        functools.partial(main_kernel, slice_rows, len(pieces), scale),
        out_shape=jax.ShapeDtypeStruct((parts, modes // parts, 3 * modes), F32),
        in_specs=[SMEM, SMEM, SMEM, SMEM, VMEM, VMEM, VMEM] + [VMEM] * len(pieces),
        out_specs=VMEM,
        scratch_shapes=[
            wide(2 * total), wide(count), wide(count), wide(2 * n_blocks * size),
            pltpu.VMEM((2 * modes, 2 * LANES), F32), pltpu.VMEM((modes, LANES), F32),
        ],
        compiler_params=pltpu.CompilerParams(vmem_limit_bytes=56 * 2**20),
    )(bases, rim, clash, dofs, stiffness, from_left, from_right, *pieces)


def ring_pieces(packed, index, count):
    ring = count // 2
    move = lambda value, dx, dy: lax.ppermute(
        value, "blk",
        [(i, ((i // ring + dx) % 2) * ring + (i % ring + dy) % ring) for i in range(count)],
    )
    x, y = index // ring, index % ring
    base = lambda flip, dy: ((jnp.remainder(x + flip, 2)) * ring + jnp.remainder(y + dy, ring))
    own, steps, parts, split = [packed], [0], [], ring // 4
    up = down = packed
    sent = 0
    for k in range(1, ring // 2 + 1):
        up = move(up, 0, 1)
        own.append(up)
        steps.append(-k)
        if k < ring // 2:
            down = move(down, 0, -1)
            own.append(down)
            steps.append(k)
        if k == split or k == ring // 2:
            parts.append((move(jnp.concatenate(own[sent:], axis=0), 1, 0), steps[sent:]))
            sent = len(own)
    places = [base(0, dy) for dy in steps]
    for _, dys in parts:
        places += [base(1, dy) for dy in dys]
    return own + [part for part, _ in parts], jnp.stack(places).astype(jnp.int32)


def on_device(stiffness, dofmap, eigvecs, rim_rows, owner_map):
    blk_count, sub_count = lax.axis_size("blk"), lax.axis_size("sub")
    own_rows = eigvecs.shape[2]
    slice_rows = own_rows // 2
    block_count, block_size = dofmap.shape[1:]
    blk, sub = lax.axis_index("blk"), lax.axis_index("sub")
    with jax.named_scope("pack"):
        packed = pack(eigvecs[0])
    with jax.named_scope("index_words"):
        dofs, rim, clash = index_words(dofmap[0], rim_rows[0])
    with jax.named_scope("gather_modes"):
        pieces, places = ring_pieces(packed, blk, blk_count)
        bases = places * own_rows
    with jax.named_scope("rim"):
        left, right = take_rim(bases, rim, pieces, slice_rows)
        from_left = lax.ppermute(right, "sub", [(i, i + 1) for i in range(sub_count - 1)])
        from_right = lax.ppermute(left, "sub", [(i + 1, i) for i in range(sub_count - 1)])
    with jax.named_scope("contract"):
        scale = 1.0 / math.sqrt(block_count * blk_count * block_size)
        share = contract_blocks(
            bases, rim, clash, dofs, stiffness[0], from_left, from_right, pieces, slice_rows, blk_count, scale
        )
    with jax.named_scope("sum_over_blk"):
        mine = jnp.sum(lax.all_to_all(share, "blk", 0, 0, tiled=True), axis=0)
    with jax.named_scope("relay"):
        sent = jnp.broadcast_to(mine[None], (sub_count,) + mine.shape)
        arrived = lax.all_to_all(sent, "sub", 0, 0, tiled=True)
    with jax.named_scope("slots"):
        positions = jnp.arange(sub_count, dtype=jnp.int32)
        same_owner = owner_map[:, None] == owner_map[None, :]
        earlier = positions[None, :] < positions[:, None]
        slot_rank = jnp.sum((same_owner & earlier).astype(jnp.int32), axis=1)
        slot_ids = jnp.arange(CAP, dtype=jnp.int32)
        chosen = (owner_map[None, :] == sub) & (slot_rank[None, :] == slot_ids[:, None])
        none = jnp.zeros((CAP, 1), bool)
        from_prev = jnp.concatenate([chosen[:, 1:], none], axis=1)
        from_next = jnp.concatenate([none, chosen[:, :-1]], axis=1)
        modes = LANES // 2
        parts = [
            jnp.sum(jnp.where(pick[:, :, None, None], arrived[None, :, :, p * modes:(p + 1) * modes], 0.0), axis=1)
            for p, pick in enumerate((from_prev, chosen, from_next))
        ]
        return jnp.concatenate(parts, axis=2)


def solution(mesh):
    return jax.shard_map(
        on_device,
        mesh=mesh,
        in_specs=(
            P("sub", "blk", None, None),
            P("sub", "blk", None),
            P("sub", None, "blk"),
            P("sub", None, None),
            P(),
        ),
        out_specs=P("sub", "blk", None),
        check_vma=False,
    )
```

```python
import functools
import math

import jax
import jax.numpy as jnp
from jax import lax
from jax.experimental import pallas as pl
from jax.experimental.pallas import tpu as pltpu
from jax.sharding import PartitionSpec as P

CAP = 4
LANES = 128
CHUNK = 256
GROUP = 16
TOGETHER = 16
F32 = jnp.float32
BF16 = jnp.bfloat16
VMEM = pl.BlockSpec(memory_space=pltpu.VMEM)
SMEM = pl.BlockSpec(memory_space=pltpu.SMEM)


def low_lanes(rows):
    return lax.broadcasted_iota(jnp.int32, (rows, LANES), 1) < LANES // 2


def pack_kernel(modes_ref, out_ref):
    wide = modes_ref[...].astype(F32)
    half = wide.shape[1] // 2
    stacked = jnp.concatenate([wide[:, :half], wide[:, half:]], axis=0)
    out_ref[...] = stacked.T.astype(BF16)


def pack(modes):
    count, width = modes.shape
    return pl.pallas_call(
        pack_kernel,
        out_shape=jax.ShapeDtypeStruct((width // 2, 2 * count), BF16),
        in_specs=[VMEM],
        out_specs=VMEM,
        compiler_params=pltpu.CompilerParams(vmem_limit_bytes=8 * 2**20),
    )(modes)


def index_kernel(dof_ref, rim_ref, dof_words, rim_words, clash_ref):
    size = dof_ref.shape[1]
    dofs = dof_ref[...]
    dof_words[...] = 2 * dofs + (pltpu.roll(dofs, size // 2, 1) << 17)
    rows = rim_words.shape[0]
    sides = [
        jnp.concatenate([rim_ref[side:side + 1, r * LANES:(r + 1) * LANES] for r in range(rows)], axis=0)
        for side in range(2)
    ]
    rim_words[...] = 2 * sides[0] + (sides[1] << 17)
    place = lax.broadcasted_iota(jnp.int32, (rows, LANES), 1) % GROUP
    clash = jnp.zeros((rows, LANES), jnp.int32)
    for d in range(1, GROUP):
        for side in sides:
            clash = jnp.where((pltpu.roll(side, d, 1) == side) & (place >= d), 1, clash)
    step = 1
    while step < GROUP:
        clash = jnp.maximum(clash, pltpu.roll(clash, step, 1))
        step *= 2
    clash_ref[...] = clash


def index_words(dofs, rim):
    rows = rim.shape[1] // LANES
    word = lambda r, c: jax.ShapeDtypeStruct((r, c), jnp.int32)
    return pl.pallas_call(
        index_kernel,
        out_shape=(word(*dofs.shape), word(rows, LANES), word(rows, LANES)),
        in_specs=[VMEM, VMEM],
        out_specs=(VMEM, VMEM, VMEM),
        compiler_params=pltpu.CompilerParams(vmem_limit_bytes=8 * 2**20),
    )(dofs, rim)


def unpack_slices(base_ref, pieces, slice_rows, table, clear):
    at = 0
    for piece in pieces:
        for first in range(0, piece.shape[0], slice_rows):
            base = base_ref[at]
            at += 1

            def step(c, _):
                start = pl.multiple_of(c * CHUNK, CHUNK)
                wide = piece[pl.ds(first + start, CHUNK), :].astype(F32)
                low = low_lanes(CHUNK)
                here = pl.multiple_of(base + start, CHUNK)
                there = pl.multiple_of(base + slice_rows + start, CHUNK)
                turned = pltpu.roll(wide, LANES // 2, 1)
                for at_row, value in ((here, wide), (there, turned)):
                    if clear:
                        value = jnp.where(low, value, 0.0)
                        table[pl.ds(2 * at_row + 1, CHUNK, stride=2), :] = jnp.zeros_like(value)
                    table[pl.ds(2 * at_row, CHUNK, stride=2), :] = value
                return 0

            lax.fori_loop(0, slice_rows // CHUNK, step, 0)


def rim_kernel(slice_rows, n_pieces, base_ref, rim_ref, *refs):
    pieces, (left_ref, right_ref), (table, taken) = refs[:n_pieces], refs[n_pieces:n_pieces + 2], refs[n_pieces + 2:]
    unpack_slices(base_ref, pieces, slice_rows, table, False)
    groups, group = rim_ref.shape
    count = groups * group

    def gather(g, _):
        first = pl.multiple_of(g * group, group)
        to_left, to_right = taken.at[pl.ds(first, group)], taken.at[pl.ds(count + first, group)]
        for j in range(group):
            word = rim_ref[g, j]
            to_left[pl.ds(j, 1), :] = table[pl.ds(word & 0xFFFF, 1), :]
            to_right[pl.ds(j, 1), :] = table[pl.ds(word >> 16, 1), :]
        return 0

    lax.fori_loop(0, groups, gather, 0)
    half = count // 2
    for at, out in ((0, left_ref), (count, right_ref)):
        first, second = taken[at:at + half, :], taken[at + half:at + count, :]
        out[...] = jnp.where(low_lanes(half), first, pltpu.roll(second, LANES // 2, 1)).astype(BF16)


def take_rim(bases, rim, pieces, slice_rows):
    total = 2 * sum(p.shape[0] for p in pieces)
    count = rim.size
    packed = jax.ShapeDtypeStruct((count // 2, LANES), BF16)
    return pl.pallas_call(
        functools.partial(rim_kernel, slice_rows, len(pieces)),
        out_shape=(packed, packed),
        in_specs=[SMEM, SMEM] + [VMEM] * len(pieces),
        out_specs=(VMEM, VMEM),
        scratch_shapes=[pltpu.VMEM((2 * total, LANES), F32), pltpu.VMEM((2 * count, LANES), F32)],
        compiler_params=pltpu.CompilerParams(vmem_limit_bytes=28 * 2**20),
    )(bases, rim, *pieces)


def spread_rim(packed, out, high):
    half = packed.shape[0]

    def step(c, _):
        start = pl.multiple_of(c * CHUNK, CHUNK)
        wide = packed[pl.ds(start, CHUNK), :].astype(F32)
        turned = pltpu.roll(wide, LANES // 2, 1)
        low = low_lanes(CHUNK)
        if high:
            first, second = jnp.where(low, 0.0, turned), jnp.where(low, 0.0, wide)
        else:
            first, second = jnp.where(low, wide, 0.0), jnp.where(low, turned, 0.0)
        out[pl.ds(start, CHUNK), :] = first
        out[pl.ds(half + start, CHUNK), :] = second
        return 0

    lax.fori_loop(0, half // CHUNK, step, 0)


def main_kernel(
    slice_rows, n_pieces, scale, base_ref, rim_ref, clash_ref, dof_ref, stiff_ref, from_left, from_right, *refs
):
    pieces = refs[:n_pieces]
    out_ref = refs[n_pieces]
    table, rim_a, rim_b, got, acc, acc_low = refs[n_pieces + 1:]
    unpack_slices(base_ref, pieces, slice_rows, table, True)
    spread_rim(from_left, rim_a, True)
    spread_rim(from_right, rim_b, False)
    rim_groups, group_rows = rim_ref.shape

    def add_rows(g, _):
        first = pl.multiple_of(g * group_rows, group_rows)
        for k in range(0, group_rows, GROUP):
            new_a, new_b = rim_a.at[pl.ds(first + k, GROUP)], rim_b.at[pl.ds(first + k, GROUP)]

            @pl.when(clash_ref[g, k + GROUP - 1] == 0)
            def _(k=k, new_a=new_a, new_b=new_b):
                words = [rim_ref[g, k + j] for j in range(GROUP)]
                at = [(word & 0xFFFF, (word >> 16) + 1) for word in words]
                sums = [
                    (table[pl.ds(a, 1), :] + new_a[pl.ds(j, 1), :], table[pl.ds(b, 1), :] + new_b[pl.ds(j, 1), :])
                    for j, (a, b) in enumerate(at)
                ]
                for (a, b), (sum_a, sum_b) in zip(at, sums):
                    table[pl.ds(a, 1), :] = sum_a
                    table[pl.ds(b, 1), :] = sum_b

            @pl.when(clash_ref[g, k + GROUP - 1] != 0)
            def _(k=k, new_a=new_a, new_b=new_b):
                def one(j, _):
                    word = rim_ref[g, k + j]
                    table[pl.ds(word & 0xFFFF, 1), :] += new_a[pl.ds(j, 1), :]
                    table[pl.ds((word >> 16) + 1, 1), :] += new_b[pl.ds(j, 1), :]
                    return 0

                lax.fori_loop(0, GROUP, one, 0)

        return 0

    lax.fori_loop(0, rim_groups, add_rows, 0)

    n_blocks, size = dof_ref.shape
    modes = LANES // 2

    def gather(e, _):
        to = got.at[pl.ds(pl.multiple_of(2 * e * size, 2 * size), 2 * size)]
        for j in range(size // 2):
            word = dof_ref[e, j]
            to[pl.ds(2 * j, 2), :] = table[pl.ds(word & 0xFFFF, 2), :]
            to[pl.ds(size + 2 * j, 2), :] = table[pl.ds(word >> 16, 2), :]
        return 0

    lax.fori_loop(0, n_blocks, gather, 0)

    acc[...] = jnp.zeros_like(acc)
    acc_low[...] = jnp.zeros_like(acc_low)
    width = TOGETHER * size

    def contract(i, _):
        first = pl.multiple_of(2 * i * width, 2 * width)
        wide_a, wide_b = got[pl.ds(first, width, stride=2), :], got[pl.ds(first + 1, width, stride=2), :]
        high_a, high_b = wide_a.astype(BF16), wide_b.astype(BF16)
        low_ab = ((wide_a - high_a.astype(F32)) + (wide_b - high_b.astype(F32))).astype(BF16)
        picked = high_a.T[:modes, :]
        image = jnp.concatenate(
            [
                jnp.dot(picked[:, e * size:(e + 1) * size], stiff_ref[i * TOGETHER + e], preferred_element_type=F32)
                for e in range(TOGETHER)
            ],
            axis=1,
        )
        image_high = image.astype(BF16)
        image_low = (image - image_high.astype(F32)).astype(BF16)
        both = jnp.concatenate([image_high, image_low], axis=0)
        right = jnp.concatenate([high_a, high_b], axis=1)
        acc[...] += jnp.dot(both, right, preferred_element_type=F32)
        acc_low[...] += jnp.dot(image_high, low_ab, preferred_element_type=F32)
        return 0

    lax.fori_loop(0, n_blocks // TOGETHER, contract, 0)
    summed = acc[:modes, :] + acc[modes:, :]
    first, second = summed[:, :LANES], summed[:, LANES:]
    rest = acc_low[...]
    low = low_lanes(modes)
    first = first + jnp.where(low, 0.0, rest)
    second = second + jnp.where(low, rest, 0.0)
    first_t, second_t = (first * scale).T, (second * scale).T
    own, to_prev, to_next = first_t[:modes], first_t[modes:], second_t[:modes]
    rows = jnp.concatenate([to_next, own, to_prev], axis=1)
    share = out_ref.shape[1]
    for d in range(out_ref.shape[0]):
        out_ref[d] = rows[d * share:(d + 1) * share]


def contract_blocks(bases, rim, clash, dofs, stiffness, from_left, from_right, pieces, slice_rows, parts, scale):
    total = 2 * sum(p.shape[0] for p in pieces)
    count = rim.size
    modes = LANES // 2
    n_blocks, size = dofs.shape
    wide = lambda n: pltpu.VMEM((n, LANES), F32)
    return pl.pallas_call(
        functools.partial(main_kernel, slice_rows, len(pieces), scale),
        out_shape=jax.ShapeDtypeStruct((parts, modes // parts, 3 * modes), F32),
        in_specs=[SMEM, SMEM, SMEM, SMEM, VMEM, VMEM, VMEM] + [VMEM] * len(pieces),
        out_specs=VMEM,
        scratch_shapes=[
            wide(2 * total), wide(count), wide(count), wide(2 * n_blocks * size),
            pltpu.VMEM((2 * modes, 2 * LANES), F32), pltpu.VMEM((modes, LANES), F32),
        ],
        compiler_params=pltpu.CompilerParams(vmem_limit_bytes=44 * 2**20),
    )(bases, rim, clash, dofs, stiffness, from_left, from_right, *pieces)


def slots_kernel(me_ref, owner_ref, arrived_ref, out_ref):
    count = arrived_ref.shape[0]
    shape = arrived_ref.shape[1:]
    part = lax.broadcasted_iota(jnp.int32, shape, 1) // (LANES // 2)
    out_ref[...] = jnp.zeros_like(out_ref)

    def step(t, slot):
        mine = owner_ref[t] == me_ref[0]

        @pl.when(mine)
        def _():
            before = jnp.where(t > 0, arrived_ref[jnp.maximum(t - 1, 0)], 0.0)
            after = jnp.where(t < count - 1, arrived_ref[jnp.minimum(t + 1, count - 1)], 0.0)
            row = jnp.where(part == 0, before, jnp.where(part == 1, arrived_ref[t], after))
            out_ref[jnp.minimum(slot, CAP - 1)] = row

        return slot + mine.astype(jnp.int32)

    lax.fori_loop(0, count, step, 0)


def fill_slots(me, owner_map, arrived):
    return pl.pallas_call(
        slots_kernel,
        out_shape=jax.ShapeDtypeStruct((CAP,) + arrived.shape[1:], F32),
        in_specs=[SMEM, SMEM, VMEM],
        out_specs=VMEM,
        compiler_params=pltpu.CompilerParams(vmem_limit_bytes=8 * 2**20),
    )(me.astype(jnp.int32), owner_map, arrived)


def ring_pieces(packed, index, count, beside):
    ring = count // 2
    move = lambda value, dx, dy: lax.ppermute(
        value, "blk",
        [(i, ((i // ring + dx) % 2) * ring + (i % ring + dy) % ring) for i in range(count)],
    )
    x, y = index // ring, index % ring
    base = lambda flip, dy: ((jnp.remainder(x + flip, 2)) * ring + jnp.remainder(y + dy, ring))
    rows = packed.shape[0]
    both = jnp.concatenate([packed, move(packed, 1, 0)], axis=0)
    both, beside = lax.optimization_barrier((both, beside))
    pieces, places = [both], [base(0, 0), base(1, 0)]
    up = down = both
    for k in range(1, ring // 2):
        up, down = move(up, 0, 1), move(down, 0, -1)
        pieces += [up, down]
        places += [base(0, -k), base(1, -k), base(0, k), base(1, k)]
    pieces += [move(up[:rows], 0, 1), move(down[rows:], 0, -1)]
    places += [base(0, ring // 2), base(1, ring // 2)]
    return pieces, jnp.stack(places).astype(jnp.int32), beside


def on_device(stiffness, dofmap, eigvecs, rim_rows, owner_map):
    blk_count, sub_count = lax.axis_size("blk"), lax.axis_size("sub")
    own_rows = eigvecs.shape[2]
    slice_rows = own_rows // 2
    block_count, block_size = dofmap.shape[1:]
    blk, sub = lax.axis_index("blk"), lax.axis_index("sub")
    with jax.named_scope("pack"):
        packed = pack(eigvecs[0])
    with jax.named_scope("index_words"):
        dofs, rim, clash = index_words(dofmap[0], lax.optimization_barrier((rim_rows[0], packed))[0])
    with jax.named_scope("gather_modes"):
        pieces, places, (dofs, rim, clash) = ring_pieces(packed, blk, blk_count, (dofs, rim, clash))
        bases = places * own_rows
    with jax.named_scope("rim"):
        left, right = take_rim(bases, rim, pieces, slice_rows)
        from_left = lax.ppermute(right, "sub", [(i, i + 1) for i in range(sub_count - 1)])
        from_right = lax.ppermute(left, "sub", [(i + 1, i) for i in range(sub_count - 1)])
    with jax.named_scope("contract"):
        scale = 1.0 / math.sqrt(block_count * blk_count * block_size)
        share = contract_blocks(
            bases, rim, clash, dofs, stiffness[0], from_left, from_right, pieces, slice_rows, blk_count, scale
        )
    with jax.named_scope("sum_over_blk"):
        mine = jnp.sum(lax.all_to_all(share, "blk", 0, 0, tiled=True), axis=0)
    with jax.named_scope("relay"):
        sent = jnp.broadcast_to(mine[None], (sub_count,) + mine.shape)
        arrived = lax.all_to_all(sent, "sub", 0, 0, tiled=True)
    with jax.named_scope("slots"):
        return fill_slots(jnp.reshape(sub, (1,)), owner_map, arrived)


def solution(mesh):
    return jax.shard_map(
        on_device,
        mesh=mesh,
        in_specs=(
            P("sub", "blk", None, None),
            P("sub", "blk", None),
            P("sub", None, "blk"),
            P("sub", None, None),
            P(),
        ),
        out_specs=P("sub", "blk", None),
        check_vma=False,
    )
```

```python
import functools
import math

import jax
import jax.numpy as jnp
from jax import lax
from jax.experimental import pallas as pl
from jax.experimental.pallas import tpu as pltpu
from jax.sharding import PartitionSpec as P

CAP = 4
LANES = 128
CHUNK = 256
GROUP = 16
TOGETHER = 16
F32 = jnp.float32
BF16 = jnp.bfloat16
VMEM = pl.BlockSpec(memory_space=pltpu.VMEM)
SMEM = pl.BlockSpec(memory_space=pltpu.SMEM)


def low_lanes(rows):
    return lax.broadcasted_iota(jnp.int32, (rows, LANES), 1) < LANES // 2


def pack_kernel(modes_ref, out_ref):
    wide = modes_ref[...].astype(F32)
    half = wide.shape[1] // 2
    stacked = jnp.concatenate([wide[:, :half], wide[:, half:]], axis=0)
    out_ref[...] = stacked.T.astype(BF16)


def pack(modes):
    count, width = modes.shape
    return pl.pallas_call(
        pack_kernel,
        out_shape=jax.ShapeDtypeStruct((width // 2, 2 * count), BF16),
        in_specs=[VMEM],
        out_specs=VMEM,
        compiler_params=pltpu.CompilerParams(vmem_limit_bytes=8 * 2**20),
    )(modes)


def index_kernel(dof_ref, rim_ref, dof_words, rim_words, clash_ref):
    size = dof_ref.shape[1]
    dofs = dof_ref[...]
    dof_words[...] = 2 * dofs + (pltpu.roll(dofs, size // 2, 1) << 17)
    rows = rim_words.shape[0]
    sides = [
        jnp.concatenate([rim_ref[side:side + 1, r * LANES:(r + 1) * LANES] for r in range(rows)], axis=0)
        for side in range(2)
    ]
    rim_words[...] = 2 * sides[0] + (sides[1] << 17)
    place = lax.broadcasted_iota(jnp.int32, (rows, LANES), 1) % GROUP
    clash = jnp.zeros((rows, LANES), jnp.int32)
    for d in range(1, GROUP):
        for side in sides:
            clash = jnp.where((pltpu.roll(side, d, 1) == side) & (place >= d), 1, clash)
    step = 1
    while step < GROUP:
        clash = jnp.maximum(clash, pltpu.roll(clash, step, 1))
        step *= 2
    clash_ref[...] = clash


def index_words(dofs, rim):
    rows = rim.shape[1] // LANES
    word = lambda r, c: jax.ShapeDtypeStruct((r, c), jnp.int32)
    return pl.pallas_call(
        index_kernel,
        out_shape=(word(*dofs.shape), word(rows, LANES), word(rows, LANES)),
        in_specs=[VMEM, VMEM],
        out_specs=(VMEM, VMEM, VMEM),
        compiler_params=pltpu.CompilerParams(vmem_limit_bytes=8 * 2**20),
    )(dofs, rim)


def unpack_slices(base_ref, pieces, slice_rows, table, clear):
    at = 0
    for piece in pieces:
        for first in range(0, piece.shape[0], slice_rows):
            base = base_ref[at]
            at += 1

            def step(c, _):
                start = pl.multiple_of(c * CHUNK, CHUNK)
                wide = piece[pl.ds(first + start, CHUNK), :].astype(F32)
                low = low_lanes(CHUNK)
                here = pl.multiple_of(base + start, CHUNK)
                there = pl.multiple_of(base + slice_rows + start, CHUNK)
                turned = pltpu.roll(wide, LANES // 2, 1)
                for at_row, value in ((here, wide), (there, turned)):
                    if clear:
                        value = jnp.where(low, value, 0.0)
                        table[pl.ds(2 * at_row + 1, CHUNK, stride=2), :] = jnp.zeros_like(value)
                    table[pl.ds(2 * at_row, CHUNK, stride=2), :] = value
                return 0

            lax.fori_loop(0, slice_rows // CHUNK, step, 0)


def rim_kernel(slice_rows, n_pieces, base_ref, rim_ref, *refs):
    pieces, (left_ref, right_ref), (table, taken) = refs[:n_pieces], refs[n_pieces:n_pieces + 2], refs[n_pieces + 2:]
    unpack_slices(base_ref, pieces, slice_rows, table, False)
    groups, group = rim_ref.shape
    count = groups * group

    def gather(g, _):
        first = pl.multiple_of(g * group, group)
        to_left, to_right = taken.at[pl.ds(first, group)], taken.at[pl.ds(count + first, group)]
        for j in range(group):
            word = rim_ref[g, j]
            to_left[pl.ds(j, 1), :] = table[pl.ds(word & 0xFFFF, 1), :]
            to_right[pl.ds(j, 1), :] = table[pl.ds(word >> 16, 1), :]
        return 0

    lax.fori_loop(0, groups, gather, 0)
    half = count // 2
    for at, out in ((0, left_ref), (count, right_ref)):
        first, second = taken[at:at + half, :], taken[at + half:at + count, :]
        out[...] = jnp.where(low_lanes(half), first, pltpu.roll(second, LANES // 2, 1)).astype(BF16)


def take_rim(bases, rim, pieces, slice_rows):
    total = 2 * sum(p.shape[0] for p in pieces)
    count = rim.size
    packed = jax.ShapeDtypeStruct((count // 2, LANES), BF16)
    return pl.pallas_call(
        functools.partial(rim_kernel, slice_rows, len(pieces)),
        out_shape=(packed, packed),
        in_specs=[SMEM, SMEM] + [VMEM] * len(pieces),
        out_specs=(VMEM, VMEM),
        scratch_shapes=[pltpu.VMEM((2 * total, LANES), F32), pltpu.VMEM((2 * count, LANES), F32)],
        compiler_params=pltpu.CompilerParams(vmem_limit_bytes=28 * 2**20),
    )(bases, rim, *pieces)


def spread_rim(packed, out, high):
    half = packed.shape[0]

    def step(c, _):
        start = pl.multiple_of(c * CHUNK, CHUNK)
        wide = packed[pl.ds(start, CHUNK), :].astype(F32)
        turned = pltpu.roll(wide, LANES // 2, 1)
        low = low_lanes(CHUNK)
        if high:
            first, second = jnp.where(low, 0.0, turned), jnp.where(low, 0.0, wide)
        else:
            first, second = jnp.where(low, wide, 0.0), jnp.where(low, turned, 0.0)
        out[pl.ds(start, CHUNK), :] = first
        out[pl.ds(half + start, CHUNK), :] = second
        return 0

    lax.fori_loop(0, half // CHUNK, step, 0)


def main_kernel(
    slice_rows, n_pieces, scale, base_ref, rim_ref, clash_ref, dof_ref, stiff_hbm, from_left, from_right, *refs
):
    pieces = refs[:n_pieces]
    out_ref = refs[n_pieces]
    table, rim_a, rim_b, got, acc, acc_low, stiff_ref, arrived = refs[n_pieces + 1:]
    fetch = pltpu.make_async_copy(stiff_hbm, stiff_ref, arrived)
    fetch.start()
    unpack_slices(base_ref, pieces, slice_rows, table, True)
    spread_rim(from_left, rim_a, True)
    spread_rim(from_right, rim_b, False)
    rim_groups, group_rows = rim_ref.shape

    def add_rows(g, _):
        first = pl.multiple_of(g * group_rows, group_rows)
        for k in range(0, group_rows, GROUP):
            new_a, new_b = rim_a.at[pl.ds(first + k, GROUP)], rim_b.at[pl.ds(first + k, GROUP)]

            @pl.when(clash_ref[g, k + GROUP - 1] == 0)
            def _(k=k, new_a=new_a, new_b=new_b):
                words = [rim_ref[g, k + j] for j in range(GROUP)]
                at = [(word & 0xFFFF, (word >> 16) + 1) for word in words]
                sums = [
                    (table[pl.ds(a, 1), :] + new_a[pl.ds(j, 1), :], table[pl.ds(b, 1), :] + new_b[pl.ds(j, 1), :])
                    for j, (a, b) in enumerate(at)
                ]
                for (a, b), (sum_a, sum_b) in zip(at, sums):
                    table[pl.ds(a, 1), :] = sum_a
                    table[pl.ds(b, 1), :] = sum_b

            @pl.when(clash_ref[g, k + GROUP - 1] != 0)
            def _(k=k, new_a=new_a, new_b=new_b):
                def one(j, _):
                    word = rim_ref[g, k + j]
                    table[pl.ds(word & 0xFFFF, 1), :] += new_a[pl.ds(j, 1), :]
                    table[pl.ds((word >> 16) + 1, 1), :] += new_b[pl.ds(j, 1), :]
                    return 0

                lax.fori_loop(0, GROUP, one, 0)

        return 0

    lax.fori_loop(0, rim_groups, add_rows, 0)

    n_blocks, size = dof_ref.shape
    modes = LANES // 2

    def gather(e, _):
        to = got.at[pl.ds(pl.multiple_of(2 * e * size, 2 * size), 2 * size)]
        for j in range(size // 2):
            word = dof_ref[e, j]
            to[pl.ds(2 * j, 2), :] = table[pl.ds(word & 0xFFFF, 2), :]
            to[pl.ds(size + 2 * j, 2), :] = table[pl.ds(word >> 16, 2), :]
        return 0

    lax.fori_loop(0, n_blocks, gather, 0)

    fetch.wait()
    acc[...] = jnp.zeros_like(acc)
    acc_low[...] = jnp.zeros_like(acc_low)
    width = TOGETHER * size

    def contract(i, _):
        first = pl.multiple_of(2 * i * width, 2 * width)
        wide_a, wide_b = got[pl.ds(first, width, stride=2), :], got[pl.ds(first + 1, width, stride=2), :]
        high_a, high_b = wide_a.astype(BF16), wide_b.astype(BF16)
        low_ab = ((wide_a - high_a.astype(F32)) + (wide_b - high_b.astype(F32))).astype(BF16)
        picked = high_a.T[:modes, :]
        image = jnp.concatenate(
            [
                jnp.dot(picked[:, e * size:(e + 1) * size], stiff_ref[i * TOGETHER + e], preferred_element_type=F32)
                for e in range(TOGETHER)
            ],
            axis=1,
        )
        image_high = image.astype(BF16)
        image_low = (image - image_high.astype(F32)).astype(BF16)
        both = jnp.concatenate([image_high, image_low], axis=0)
        right = jnp.concatenate([high_a, high_b], axis=1)
        acc[...] += jnp.dot(both, right, preferred_element_type=F32)
        acc_low[...] += jnp.dot(image_high, low_ab, preferred_element_type=F32)
        return 0

    lax.fori_loop(0, n_blocks // TOGETHER, contract, 0)
    summed = acc[:modes, :] + acc[modes:, :]
    first, second = summed[:, :LANES], summed[:, LANES:]
    rest = acc_low[...]
    low = low_lanes(modes)
    first = first + jnp.where(low, 0.0, rest)
    second = second + jnp.where(low, rest, 0.0)
    first_t, second_t = (first * scale).T, (second * scale).T
    own, to_prev, to_next = first_t[:modes], first_t[modes:], second_t[:modes]
    rows = jnp.concatenate([to_next, own, to_prev], axis=1)
    share = out_ref.shape[1]
    for d in range(out_ref.shape[0]):
        out_ref[d] = rows[d * share:(d + 1) * share]


def contract_blocks(bases, rim, clash, dofs, stiffness, from_left, from_right, pieces, slice_rows, parts, scale):
    total = 2 * sum(p.shape[0] for p in pieces)
    count = rim.size
    modes = LANES // 2
    n_blocks, size = dofs.shape
    wide = lambda n: pltpu.VMEM((n, LANES), F32)
    return pl.pallas_call(
        functools.partial(main_kernel, slice_rows, len(pieces), scale),
        out_shape=jax.ShapeDtypeStruct((parts, modes // parts, 3 * modes), F32),
        in_specs=[SMEM] * 4 + [pl.BlockSpec(memory_space=pltpu.HBM)] + [VMEM] * (2 + len(pieces)),
        out_specs=VMEM,
        scratch_shapes=[
            wide(2 * total), wide(count), wide(count), wide(2 * n_blocks * size),
            pltpu.VMEM((2 * modes, 2 * LANES), F32), pltpu.VMEM((modes, LANES), F32),
            pltpu.VMEM(stiffness.shape, BF16), pltpu.SemaphoreType.DMA,
        ],
        compiler_params=pltpu.CompilerParams(vmem_limit_bytes=50 * 2**20),
    )(bases, rim, clash, dofs, stiffness, from_left, from_right, *pieces)


def slots_kernel(me_ref, owner_ref, arrived_ref, out_ref):
    count = arrived_ref.shape[0]
    shape = arrived_ref.shape[1:]
    part = lax.broadcasted_iota(jnp.int32, shape, 1) // (LANES // 2)
    out_ref[...] = jnp.zeros_like(out_ref)

    def step(t, slot):
        mine = owner_ref[t] == me_ref[0]

        @pl.when(mine)
        def _():
            before = jnp.where(t > 0, arrived_ref[jnp.maximum(t - 1, 0)], 0.0)
            after = jnp.where(t < count - 1, arrived_ref[jnp.minimum(t + 1, count - 1)], 0.0)
            row = jnp.where(part == 0, before, jnp.where(part == 1, arrived_ref[t], after))
            out_ref[jnp.minimum(slot, CAP - 1)] = row

        return slot + mine.astype(jnp.int32)

    lax.fori_loop(0, count, step, 0)


def fill_slots(me, owner_map, arrived):
    return pl.pallas_call(
        slots_kernel,
        out_shape=jax.ShapeDtypeStruct((CAP,) + arrived.shape[1:], F32),
        in_specs=[SMEM, SMEM, VMEM],
        out_specs=VMEM,
        compiler_params=pltpu.CompilerParams(vmem_limit_bytes=8 * 2**20),
    )(me.astype(jnp.int32), owner_map, arrived)


def ring_pieces(packed, index, count, beside):
    ring = count // 2
    move = lambda value, dx, dy: lax.ppermute(
        value, "blk",
        [(i, ((i // ring + dx) % 2) * ring + (i % ring + dy) % ring) for i in range(count)],
    )
    x, y = index // ring, index % ring
    base = lambda flip, dy: ((jnp.remainder(x + flip, 2)) * ring + jnp.remainder(y + dy, ring))
    both = jnp.concatenate([packed, move(packed, 1, 0)], axis=0)
    both, beside = lax.optimization_barrier((both, beside))
    pieces, places = [both], [base(0, 0), base(1, 0)]
    up = down = both
    for k in range(1, ring // 2):
        up, down = move(up, 0, 1), move(down, 0, -1)
        pieces += [up, down]
        places += [base(0, -k), base(1, -k), base(0, k), base(1, k)]
    pieces.append(move(up, 0, 1))
    places += [base(0, -(ring // 2)), base(1, -(ring // 2))]
    return pieces, jnp.stack(places).astype(jnp.int32), beside


def on_device(stiffness, dofmap, eigvecs, rim_rows, owner_map):
    blk_count, sub_count = lax.axis_size("blk"), lax.axis_size("sub")
    own_rows = eigvecs.shape[2]
    slice_rows = own_rows // 2
    block_count, block_size = dofmap.shape[1:]
    blk, sub = lax.axis_index("blk"), lax.axis_index("sub")
    with jax.named_scope("pack"):
        packed = pack(eigvecs[0])
    with jax.named_scope("index_words"):
        dofs, rim, clash = index_words(dofmap[0], lax.optimization_barrier((rim_rows[0], packed))[0])
    with jax.named_scope("gather_modes"):
        pieces, places, (dofs, rim, clash) = ring_pieces(packed, blk, blk_count, (dofs, rim, clash))
        bases = places * own_rows
    with jax.named_scope("rim"):
        left, right = take_rim(bases, rim, pieces, slice_rows)
        from_left = lax.ppermute(right, "sub", [(i, i + 1) for i in range(sub_count - 1)])
        from_right = lax.ppermute(left, "sub", [(i + 1, i) for i in range(sub_count - 1)])
    with jax.named_scope("contract"):
        scale = 1.0 / math.sqrt(block_count * blk_count * block_size)
        share = contract_blocks(
            bases, rim, clash, dofs, stiffness[0], from_left, from_right, pieces, slice_rows, blk_count, scale
        )
    with jax.named_scope("sum_over_blk"):
        mine = jnp.sum(lax.all_to_all(share, "blk", 0, 0, tiled=True), axis=0)
    with jax.named_scope("relay"):
        sent = jnp.broadcast_to(mine[None], (sub_count,) + mine.shape)
        arrived = lax.all_to_all(sent, "sub", 0, 0, tiled=True)
    with jax.named_scope("slots"):
        return fill_slots(jnp.reshape(sub, (1,)), owner_map, arrived)


def solution(mesh):
    return jax.shard_map(
        on_device,
        mesh=mesh,
        in_specs=(
            P("sub", "blk", None, None),
            P("sub", "blk", None),
            P("sub", None, "blk"),
            P("sub", None, None),
            P(),
        ),
        out_specs=P("sub", "blk", None),
        check_vma=False,
    )
```

```python
import functools
import math

import jax
import jax.numpy as jnp
from jax import lax
from jax.experimental import pallas as pl
from jax.experimental.pallas import tpu as pltpu
from jax.sharding import PartitionSpec as P

CAP = 4
LANES = 128
CHUNK = 256
GROUP = 16
TOGETHER = 16
F32 = jnp.float32
BF16 = jnp.bfloat16
VMEM = pl.BlockSpec(memory_space=pltpu.VMEM)
SMEM = pl.BlockSpec(memory_space=pltpu.SMEM)


def low_lanes(rows):
    return lax.broadcasted_iota(jnp.int32, (rows, LANES), 1) < LANES // 2


def pack_kernel(modes_ref, out_ref):
    wide = modes_ref[...].astype(F32)
    half = wide.shape[1] // 2
    stacked = jnp.concatenate([wide[:, :half], wide[:, half:]], axis=0)
    out_ref[...] = stacked.T.astype(BF16)


def pack(modes):
    count, width = modes.shape
    return pl.pallas_call(
        pack_kernel,
        out_shape=jax.ShapeDtypeStruct((width // 2, 2 * count), BF16),
        in_specs=[VMEM],
        out_specs=VMEM,
        compiler_params=pltpu.CompilerParams(vmem_limit_bytes=8 * 2**20),
    )(modes)


def index_kernel(dof_ref, rim_ref, dof_words, rim_words, clash_ref):
    size = dof_ref.shape[1]
    dofs = dof_ref[...]
    dof_words[...] = 2 * dofs + (pltpu.roll(dofs, size // 2, 1) << 17)
    rows = rim_words.shape[0]
    sides = [
        jnp.concatenate([rim_ref[side:side + 1, r * LANES:(r + 1) * LANES] for r in range(rows)], axis=0)
        for side in range(2)
    ]
    rim_words[...] = 2 * sides[0] + (sides[1] << 17)
    place = lax.broadcasted_iota(jnp.int32, (rows, LANES), 1) % GROUP
    clash = jnp.zeros((rows, LANES), jnp.int32)
    for d in range(1, GROUP):
        for side in sides:
            clash = jnp.where((pltpu.roll(side, d, 1) == side) & (place >= d), 1, clash)
    step = 1
    while step < GROUP:
        clash = jnp.maximum(clash, pltpu.roll(clash, step, 1))
        step *= 2
    clash_ref[...] = clash


def index_words(dofs, rim):
    rows = rim.shape[1] // LANES
    word = lambda r, c: jax.ShapeDtypeStruct((r, c), jnp.int32)
    return pl.pallas_call(
        index_kernel,
        out_shape=(word(*dofs.shape), word(rows, LANES), word(rows, LANES)),
        in_specs=[VMEM, VMEM],
        out_specs=(VMEM, VMEM, VMEM),
        compiler_params=pltpu.CompilerParams(vmem_limit_bytes=8 * 2**20),
    )(dofs, rim)


def unpack_slices(base_ref, pieces, slice_rows, table, clear):
    at = 0
    for piece in pieces:
        for first in range(0, piece.shape[0], slice_rows):
            base = base_ref[at]
            at += 1

            def step(c, _):
                start = pl.multiple_of(c * CHUNK, CHUNK)
                wide = piece[pl.ds(first + start, CHUNK), :].astype(F32)
                low = low_lanes(CHUNK)
                here = pl.multiple_of(base + start, CHUNK)
                there = pl.multiple_of(base + slice_rows + start, CHUNK)
                turned = pltpu.roll(wide, LANES // 2, 1)
                for at_row, value in ((here, wide), (there, turned)):
                    if clear:
                        value = jnp.where(low, value, 0.0)
                        table[pl.ds(2 * at_row + 1, CHUNK, stride=2), :] = jnp.zeros_like(value)
                    table[pl.ds(2 * at_row, CHUNK, stride=2), :] = value
                return 0

            lax.fori_loop(0, slice_rows // CHUNK, step, 0)


def rim_kernel(slice_rows, n_pieces, base_ref, rim_ref, *refs):
    pieces, (left_ref, right_ref), (table, taken) = refs[:n_pieces], refs[n_pieces:n_pieces + 2], refs[n_pieces + 2:]
    unpack_slices(base_ref, pieces, slice_rows, table, False)
    groups, group = rim_ref.shape
    count = groups * group

    def gather(g, _):
        first = pl.multiple_of(g * group, group)
        to_left, to_right = taken.at[pl.ds(first, group)], taken.at[pl.ds(count + first, group)]
        for j in range(group):
            word = rim_ref[g, j]
            to_left[pl.ds(j, 1), :] = table[pl.ds(word & 0xFFFF, 1), :]
            to_right[pl.ds(j, 1), :] = table[pl.ds(word >> 16, 1), :]
        return 0

    lax.fori_loop(0, groups, gather, 0)
    half = count // 2
    for at, out in ((0, left_ref), (count, right_ref)):
        first, second = taken[at:at + half, :], taken[at + half:at + count, :]
        out[...] = jnp.where(low_lanes(half), first, pltpu.roll(second, LANES // 2, 1)).astype(BF16)


def take_rim(bases, rim, pieces, slice_rows):
    total = 2 * sum(p.shape[0] for p in pieces)
    count = rim.size
    packed = jax.ShapeDtypeStruct((count // 2, LANES), BF16)
    return pl.pallas_call(
        functools.partial(rim_kernel, slice_rows, len(pieces)),
        out_shape=(packed, packed),
        in_specs=[SMEM, SMEM] + [VMEM] * len(pieces),
        out_specs=(VMEM, VMEM),
        scratch_shapes=[pltpu.VMEM((2 * total, LANES), F32), pltpu.VMEM((2 * count, LANES), F32)],
        compiler_params=pltpu.CompilerParams(vmem_limit_bytes=28 * 2**20),
    )(bases, rim, *pieces)


def spread_rim(packed, out, high):
    half = packed.shape[0]

    def step(c, _):
        start = pl.multiple_of(c * CHUNK, CHUNK)
        wide = packed[pl.ds(start, CHUNK), :].astype(F32)
        turned = pltpu.roll(wide, LANES // 2, 1)
        low = low_lanes(CHUNK)
        if high:
            first, second = jnp.where(low, 0.0, turned), jnp.where(low, 0.0, wide)
        else:
            first, second = jnp.where(low, wide, 0.0), jnp.where(low, turned, 0.0)
        out[pl.ds(start, CHUNK), :] = first
        out[pl.ds(half + start, CHUNK), :] = second
        return 0

    lax.fori_loop(0, half // CHUNK, step, 0)


def main_kernel(
    slice_rows, n_pieces, scale, base_ref, rim_ref, clash_ref, dof_ref, stiff_hbm, from_left, from_right, *refs
):
    pieces = refs[:n_pieces]
    out_ref = refs[n_pieces]
    table, rim_a, rim_b, got, acc, acc_low, stiff_ref, arrived = refs[n_pieces + 1:]
    fetch = pltpu.make_async_copy(stiff_hbm, stiff_ref, arrived)
    fetch.start()
    unpack_slices(base_ref, pieces, slice_rows, table, True)
    spread_rim(from_left, rim_a, True)
    spread_rim(from_right, rim_b, False)
    rim_groups, group_rows = rim_ref.shape

    def add_group(g, first, k):
        new_a, new_b = rim_a.at[pl.ds(first + k, GROUP)], rim_b.at[pl.ds(first + k, GROUP)]
        words = [rim_ref[g, k + j] for j in range(GROUP)]
        at = [(word & 0xFFFF, (word >> 16) + 1) for word in words]
        sums = [
            (table[pl.ds(a, 1), :] + new_a[pl.ds(j, 1), :], table[pl.ds(b, 1), :] + new_b[pl.ds(j, 1), :])
            for j, (a, b) in enumerate(at)
        ]
        for (a, b), (sum_a, sum_b) in zip(at, sums):
            table[pl.ds(a, 1), :] = sum_a
            table[pl.ds(b, 1), :] = sum_b

    def add_one_by_one(g, first, k):
        def one(j, _):
            word = rim_ref[g, k + j]
            table[pl.ds(word & 0xFFFF, 1), :] += rim_a[pl.ds(first + k + j, 1), :]
            table[pl.ds((word >> 16) + 1, 1), :] += rim_b[pl.ds(first + k + j, 1), :]
            return 0

        lax.fori_loop(0, GROUP, one, 0)

    def add_rows(g, _):
        first = pl.multiple_of(g * group_rows, group_rows)
        ends = [k + GROUP - 1 for k in range(0, group_rows, GROUP)]
        worst = clash_ref[g, ends[0]]
        for end in ends[1:]:
            worst = worst | clash_ref[g, end]

        @pl.when(worst == 0)
        def _():
            for k in range(0, group_rows, GROUP):
                add_group(g, first, k)

        @pl.when(worst != 0)
        def _():
            for k in range(0, group_rows, GROUP):
                pl.when(clash_ref[g, k + GROUP - 1] == 0)(functools.partial(add_group, g, first, k))
                pl.when(clash_ref[g, k + GROUP - 1] != 0)(functools.partial(add_one_by_one, g, first, k))

        return 0

    lax.fori_loop(0, rim_groups, add_rows, 0)

    n_blocks, size = dof_ref.shape
    modes = LANES // 2

    def gather(e, _):
        to = got.at[pl.ds(pl.multiple_of(2 * e * size, 2 * size), 2 * size)]
        for j in range(size // 2):
            word = dof_ref[e, j]
            to[pl.ds(2 * j, 2), :] = table[pl.ds(word & 0xFFFF, 2), :]
            to[pl.ds(size + 2 * j, 2), :] = table[pl.ds(word >> 16, 2), :]
        return 0

    lax.fori_loop(0, n_blocks, gather, 0)

    fetch.wait()
    acc[...] = jnp.zeros_like(acc)
    acc_low[...] = jnp.zeros_like(acc_low)
    width = TOGETHER * size

    def contract(i, _):
        first = pl.multiple_of(2 * i * width, 2 * width)
        wide_a, wide_b = got[pl.ds(first, width, stride=2), :], got[pl.ds(first + 1, width, stride=2), :]
        high_a, high_b = wide_a.astype(BF16), wide_b.astype(BF16)
        low_ab = ((wide_a - high_a.astype(F32)) + (wide_b - high_b.astype(F32))).astype(BF16)
        picked = high_a.T[:modes, :]
        image = jnp.concatenate(
            [
                jnp.dot(picked[:, e * size:(e + 1) * size], stiff_ref[i * TOGETHER + e], preferred_element_type=F32)
                for e in range(TOGETHER)
            ],
            axis=1,
        )
        image_high = image.astype(BF16)
        image_low = (image - image_high.astype(F32)).astype(BF16)
        both = jnp.concatenate([image_high, image_low], axis=0)
        right = jnp.concatenate([high_a, high_b], axis=1)
        acc[...] += jnp.dot(both, right, preferred_element_type=F32)
        acc_low[...] += jnp.dot(image_high, low_ab, preferred_element_type=F32)
        return 0

    lax.fori_loop(0, n_blocks // TOGETHER, contract, 0)
    summed = acc[:modes, :] + acc[modes:, :]
    first, second = summed[:, :LANES], summed[:, LANES:]
    rest = acc_low[...]
    low = low_lanes(modes)
    first = first + jnp.where(low, 0.0, rest)
    second = second + jnp.where(low, rest, 0.0)
    first_t, second_t = (first * scale).T, (second * scale).T
    own, to_prev, to_next = first_t[:modes], first_t[modes:], second_t[:modes]
    rows = jnp.concatenate([to_next, own, to_prev], axis=1)
    share = out_ref.shape[1]
    for d in range(out_ref.shape[0]):
        out_ref[d] = rows[d * share:(d + 1) * share]


def contract_blocks(bases, rim, clash, dofs, stiffness, from_left, from_right, pieces, slice_rows, parts, scale):
    total = 2 * sum(p.shape[0] for p in pieces)
    count = rim.size
    modes = LANES // 2
    n_blocks, size = dofs.shape
    wide = lambda n: pltpu.VMEM((n, LANES), F32)
    return pl.pallas_call(
        functools.partial(main_kernel, slice_rows, len(pieces), scale),
        out_shape=jax.ShapeDtypeStruct((parts, modes // parts, 3 * modes), F32),
        in_specs=[SMEM] * 4 + [pl.BlockSpec(memory_space=pltpu.HBM)] + [VMEM] * (2 + len(pieces)),
        out_specs=VMEM,
        scratch_shapes=[
            wide(2 * total), wide(count), wide(count), wide(2 * n_blocks * size),
            pltpu.VMEM((2 * modes, 2 * LANES), F32), pltpu.VMEM((modes, LANES), F32),
            pltpu.VMEM(stiffness.shape, BF16), pltpu.SemaphoreType.DMA,
        ],
        compiler_params=pltpu.CompilerParams(vmem_limit_bytes=50 * 2**20),
    )(bases, rim, clash, dofs, stiffness, from_left, from_right, *pieces)


def sum_kernel(parts_ref, out_ref):
    total = parts_ref[0]
    for i in range(1, parts_ref.shape[0]):
        total = total + parts_ref[i]
    for i in range(out_ref.shape[0]):
        out_ref[i] = total


def sum_for_all(parts, receivers):
    return pl.pallas_call(
        sum_kernel,
        out_shape=jax.ShapeDtypeStruct((receivers,) + parts.shape[1:], F32),
        in_specs=[VMEM],
        out_specs=VMEM,
        compiler_params=pltpu.CompilerParams(vmem_limit_bytes=8 * 2**20),
    )(parts)


def slots_kernel(me_ref, owner_ref, arrived_ref, out_ref):
    count = arrived_ref.shape[0]
    shape = arrived_ref.shape[1:]
    part = lax.broadcasted_iota(jnp.int32, shape, 1) // (LANES // 2)
    me = me_ref[0]
    filled = jnp.int32(0)
    held = [jnp.int32(-1)] * CAP
    for t in range(count):
        mine = owner_ref[t] == me
        held = [jnp.where(mine & (filled == slot), t, old) for slot, old in enumerate(held)]
        filled = filled + mine.astype(jnp.int32)
    for slot, t in enumerate(held):
        before = jnp.where(t > 0, arrived_ref[jnp.maximum(t - 1, 0)], 0.0)
        after = jnp.where((t >= 0) & (t < count - 1), arrived_ref[jnp.minimum(t + 1, count - 1)], 0.0)
        own = jnp.where(t >= 0, arrived_ref[jnp.maximum(t, 0)], 0.0)
        out_ref[slot] = jnp.where(part == 0, before, jnp.where(part == 1, own, after))


def fill_slots(me, owner_map, arrived):
    return pl.pallas_call(
        slots_kernel,
        out_shape=jax.ShapeDtypeStruct((CAP,) + arrived.shape[1:], F32),
        in_specs=[SMEM, SMEM, VMEM],
        out_specs=VMEM,
        compiler_params=pltpu.CompilerParams(vmem_limit_bytes=8 * 2**20),
    )(me.astype(jnp.int32), owner_map, arrived)


def ring_pieces(packed, index, count, beside):
    ring = count // 2
    move = lambda value, dx, dy: lax.ppermute(
        value, "blk",
        [(i, ((i // ring + dx) % 2) * ring + (i % ring + dy) % ring) for i in range(count)],
    )
    x, y = index // ring, index % ring
    base = lambda flip, dy: ((jnp.remainder(x + flip, 2)) * ring + jnp.remainder(y + dy, ring))
    both = jnp.concatenate([packed, move(packed, 1, 0)], axis=0)
    both, beside = lax.optimization_barrier((both, beside))
    pieces, places = [both], [base(0, 0), base(1, 0)]
    up = down = both
    for k in range(1, ring // 2):
        up, down = move(up, 0, 1), move(down, 0, -1)
        pieces += [up, down]
        places += [base(0, -k), base(1, -k), base(0, k), base(1, k)]
    pieces.append(move(up, 0, 1))
    places += [base(0, -(ring // 2)), base(1, -(ring // 2))]
    return pieces, jnp.stack(places).astype(jnp.int32), beside


def on_device(stiffness, dofmap, eigvecs, rim_rows, owner_map):
    blk_count, sub_count = lax.axis_size("blk"), lax.axis_size("sub")
    own_rows = eigvecs.shape[2]
    slice_rows = own_rows // 2
    block_count, block_size = dofmap.shape[1:]
    blk, sub = lax.axis_index("blk"), lax.axis_index("sub")
    with jax.named_scope("pack"):
        packed = pack(eigvecs[0])
    with jax.named_scope("index_words"):
        dofs, rim, clash = index_words(dofmap[0], lax.optimization_barrier((rim_rows[0], packed))[0])
    with jax.named_scope("gather_modes"):
        pieces, places, (dofs, rim, clash) = ring_pieces(packed, blk, blk_count, (dofs, rim, clash))
        bases = places * own_rows
    with jax.named_scope("rim"):
        left, right = take_rim(bases, rim, pieces, slice_rows)
        from_left = lax.ppermute(right, "sub", [(i, i + 1) for i in range(sub_count - 1)])
        from_right = lax.ppermute(left, "sub", [(i + 1, i) for i in range(sub_count - 1)])
    with jax.named_scope("contract"):
        scale = 1.0 / math.sqrt(block_count * blk_count * block_size)
        share = contract_blocks(
            bases, rim, clash, dofs, stiffness[0], from_left, from_right, pieces, slice_rows, blk_count, scale
        )
    with jax.named_scope("sum_over_blk"):
        sent = sum_for_all(lax.all_to_all(share, "blk", 0, 0, tiled=True), sub_count)
    with jax.named_scope("relay"):
        arrived = lax.all_to_all(sent, "sub", 0, 0, tiled=True)
    with jax.named_scope("slots"):
        return fill_slots(jnp.reshape(sub, (1,)), owner_map, arrived)


def solution(mesh):
    return jax.shard_map(
        on_device,
        mesh=mesh,
        in_specs=(
            P("sub", "blk", None, None),
            P("sub", "blk", None),
            P("sub", None, "blk"),
            P("sub", None, None),
            P(),
        ),
        out_specs=P("sub", "blk", None),
        check_vma=False,
    )
```

```python
import functools
import math

import jax
import jax.numpy as jnp
from jax import lax
from jax.experimental import pallas as pl
from jax.experimental.pallas import tpu as pltpu
from jax.sharding import PartitionSpec as P

CAP = 4
LANES = 128
CHUNK = 256
SPARE = 8
GROUP = 16
TOGETHER = 16
F32 = jnp.float32
BF16 = jnp.bfloat16
VMEM = pl.BlockSpec(memory_space=pltpu.VMEM)
SMEM = pl.BlockSpec(memory_space=pltpu.SMEM)


def low_lanes(rows):
    return lax.broadcasted_iota(jnp.int32, (rows, LANES), 1) < LANES // 2


def pack_kernel(modes_ref, out_ref):
    wide = modes_ref[...].astype(F32)
    half = wide.shape[1] // 2
    stacked = jnp.concatenate([wide[:, :half], wide[:, half:]], axis=0)
    out_ref[...] = stacked.T.astype(BF16)


def pack(modes):
    count, width = modes.shape
    return pl.pallas_call(
        pack_kernel,
        out_shape=jax.ShapeDtypeStruct((width // 2, 2 * count), BF16),
        in_specs=[VMEM],
        out_specs=VMEM,
        compiler_params=pltpu.CompilerParams(vmem_limit_bytes=8 * 2**20),
    )(modes)


def index_kernel(dof_ref, rim_ref, dof_words, rim_words, clash_ref):
    size = dof_ref.shape[1]
    dofs = dof_ref[...]
    dof_words[...] = 2 * dofs + (pltpu.roll(dofs, size // 2, 1) << 17)
    rows = rim_words.shape[0]
    sides = [
        jnp.concatenate([rim_ref[side:side + 1, r * LANES:(r + 1) * LANES] for r in range(rows)], axis=0)
        for side in range(2)
    ]
    rim_words[...] = 2 * sides[0] + (sides[1] << 17)
    place = lax.broadcasted_iota(jnp.int32, (rows, LANES), 1) % GROUP
    clash = jnp.zeros((rows, LANES), jnp.int32)
    for d in range(1, GROUP):
        for side in sides:
            clash = jnp.where((pltpu.roll(side, d, 1) == side) & (place >= d), 1, clash)
    step = 1
    while step < GROUP:
        clash = jnp.maximum(clash, pltpu.roll(clash, step, 1))
        step *= 2
    clash_ref[...] = clash


def index_words(dofs, rim):
    rows = rim.shape[1] // LANES
    word = lambda r, c: jax.ShapeDtypeStruct((r, c), jnp.int32)
    return pl.pallas_call(
        index_kernel,
        out_shape=(word(*dofs.shape), word(rows, LANES), word(rows, LANES)),
        in_specs=[VMEM, VMEM],
        out_specs=(VMEM, VMEM, VMEM),
        compiler_params=pltpu.CompilerParams(vmem_limit_bytes=8 * 2**20),
    )(dofs, rim)


def unpack_slices(base_ref, pieces, slice_rows, table, clear):
    at = 0
    for piece in pieces:
        for first in range(0, piece.shape[0], slice_rows):
            base = base_ref[at]
            at += 1

            def step(c, _):
                start = pl.multiple_of(c * CHUNK, CHUNK)
                wide = piece[pl.ds(first + start, CHUNK), :].astype(F32)
                low = low_lanes(CHUNK)
                here = pl.multiple_of(base + start, CHUNK)
                there = pl.multiple_of(base + slice_rows + start, CHUNK)
                turned = pltpu.roll(wide, LANES // 2, 1)
                for at_row, value in ((here, wide), (there, turned)):
                    if clear:
                        value = jnp.where(low, value, 0.0)
                        table[pl.ds(2 * at_row + 1, CHUNK, stride=2), :] = jnp.zeros_like(value)
                    table[pl.ds(2 * at_row, CHUNK, stride=2), :] = value
                return 0

            lax.fori_loop(0, slice_rows // CHUNK, step, 0)


def rim_kernel(slice_rows, n_pieces, base_ref, rim_ref, *refs):
    pieces, (left_ref, right_ref), (table, taken) = refs[:n_pieces], refs[n_pieces:n_pieces + 2], refs[n_pieces + 2:]
    unpack_slices(base_ref, pieces, slice_rows, table, False)
    groups, group = rim_ref.shape
    count = groups * group

    def gather(g, _):
        first = pl.multiple_of(g * group, group)
        to_left, to_right = taken.at[pl.ds(first, group)], taken.at[pl.ds(count + first, group)]
        for j in range(group):
            word = rim_ref[g, j]
            to_left[pl.ds(j, 1), :] = table[pl.ds(word & 0xFFFF, 1), :]
            to_right[pl.ds(j, 1), :] = table[pl.ds(word >> 16, 1), :]
        return 0

    lax.fori_loop(0, groups, gather, 0)
    half = count // 2
    for at, out in ((0, left_ref), (count, right_ref)):
        first, second = taken[at:at + half, :], taken[at + half:at + count, :]
        out[...] = jnp.where(low_lanes(half), first, pltpu.roll(second, LANES // 2, 1)).astype(BF16)


def take_rim(bases, rim, pieces, slice_rows):
    total = 2 * sum(p.shape[0] for p in pieces)
    count = rim.size
    packed = jax.ShapeDtypeStruct((count // 2, LANES), BF16)
    return pl.pallas_call(
        functools.partial(rim_kernel, slice_rows, len(pieces)),
        out_shape=(packed, packed),
        in_specs=[SMEM, SMEM] + [VMEM] * len(pieces),
        out_specs=(VMEM, VMEM),
        scratch_shapes=[pltpu.VMEM((2 * total + SPARE, LANES), F32), pltpu.VMEM((2 * count, LANES), F32)],
        compiler_params=pltpu.CompilerParams(vmem_limit_bytes=28 * 2**20),
    )(bases, rim, *pieces)


def spread_rim(packed, out, high):
    half = packed.shape[0]

    def step(c, _):
        start = pl.multiple_of(c * CHUNK, CHUNK)
        wide = packed[pl.ds(start, CHUNK), :].astype(F32)
        turned = pltpu.roll(wide, LANES // 2, 1)
        low = low_lanes(CHUNK)
        if high:
            first, second = jnp.where(low, 0.0, turned), jnp.where(low, 0.0, wide)
        else:
            first, second = jnp.where(low, wide, 0.0), jnp.where(low, turned, 0.0)
        out[pl.ds(start, CHUNK), :] = first
        out[pl.ds(half + start, CHUNK), :] = second
        return 0

    lax.fori_loop(0, half // CHUNK, step, 0)


def main_kernel(
    slice_rows, n_pieces, scale, base_ref, rim_ref, clash_ref, dof_ref, stiff_hbm, from_left, from_right, *refs
):
    pieces = refs[:n_pieces]
    out_ref = refs[n_pieces]
    table, rim_a, rim_b, got, acc, acc_low, stiff_ref, arrived = refs[n_pieces + 1:]
    fetch = pltpu.make_async_copy(stiff_hbm, stiff_ref, arrived)
    fetch.start()
    unpack_slices(base_ref, pieces, slice_rows, table, True)
    spread_rim(from_left, rim_a, True)
    spread_rim(from_right, rim_b, False)
    rim_groups, group_rows = rim_ref.shape

    def add_group(g, first, k):
        new_a, new_b = rim_a.at[pl.ds(first + k, GROUP)], rim_b.at[pl.ds(first + k, GROUP)]
        words = [rim_ref[g, k + j] for j in range(GROUP)]
        at = [(word & 0xFFFF, (word >> 16) + 1) for word in words]
        sums = [
            (table[pl.ds(a, 1), :] + new_a[pl.ds(j, 1), :], table[pl.ds(b, 1), :] + new_b[pl.ds(j, 1), :])
            for j, (a, b) in enumerate(at)
        ]
        for (a, b), (sum_a, sum_b) in zip(at, sums):
            table[pl.ds(a, 1), :] = sum_a
            table[pl.ds(b, 1), :] = sum_b

    def add_one_by_one(g, first, k):
        def one(j, _):
            word = rim_ref[g, k + j]
            table[pl.ds(word & 0xFFFF, 1), :] += rim_a[pl.ds(first + k + j, 1), :]
            table[pl.ds((word >> 16) + 1, 1), :] += rim_b[pl.ds(first + k + j, 1), :]
            return 0

        lax.fori_loop(0, GROUP, one, 0)

    def add_rows(g, _):
        first = pl.multiple_of(g * group_rows, group_rows)
        ends = [k + GROUP - 1 for k in range(0, group_rows, GROUP)]
        worst = clash_ref[g, ends[0]]
        for end in ends[1:]:
            worst = worst | clash_ref[g, end]

        @pl.when(worst == 0)
        def _():
            for k in range(0, group_rows, GROUP):
                add_group(g, first, k)

        @pl.when(worst != 0)
        def _():
            for k in range(0, group_rows, GROUP):
                pl.when(clash_ref[g, k + GROUP - 1] == 0)(functools.partial(add_group, g, first, k))
                pl.when(clash_ref[g, k + GROUP - 1] != 0)(functools.partial(add_one_by_one, g, first, k))

        return 0

    lax.fori_loop(0, rim_groups, add_rows, 0)

    n_blocks, size = dof_ref.shape
    modes = LANES // 2

    def gather(e, _):
        to = got.at[pl.ds(pl.multiple_of(2 * e * size, 2 * size), 2 * size)]
        for j in range(size // 2):
            word = dof_ref[e, j]
            to[pl.ds(2 * j, 2), :] = table[pl.ds(word & 0xFFFF, 2), :]
            to[pl.ds(size + 2 * j, 2), :] = table[pl.ds(word >> 16, 2), :]
        return 0

    lax.fori_loop(0, n_blocks, gather, 0)

    fetch.wait()
    acc[...] = jnp.zeros_like(acc)
    acc_low[...] = jnp.zeros_like(acc_low)
    width = TOGETHER * size

    def contract(i, _):
        first = pl.multiple_of(2 * i * width, 2 * width)
        wide_a, wide_b = got[pl.ds(first, width, stride=2), :], got[pl.ds(first + 1, width, stride=2), :]
        high_a, high_b = wide_a.astype(BF16), wide_b.astype(BF16)
        low_ab = ((wide_a - high_a.astype(F32)) + (wide_b - high_b.astype(F32))).astype(BF16)
        picked = high_a.T[:modes, :]
        image = jnp.concatenate(
            [
                jnp.dot(picked[:, e * size:(e + 1) * size], stiff_ref[i * TOGETHER + e], preferred_element_type=F32)
                for e in range(TOGETHER)
            ],
            axis=1,
        )
        image_high = image.astype(BF16)
        image_low = (image - image_high.astype(F32)).astype(BF16)
        both = jnp.concatenate([image_high, image_low], axis=0)
        right = jnp.concatenate([high_a, high_b], axis=1)
        acc[...] += jnp.dot(both, right, preferred_element_type=F32)
        acc_low[...] += jnp.dot(image_high, low_ab, preferred_element_type=F32)
        return 0

    lax.fori_loop(0, n_blocks // TOGETHER, contract, 0)
    summed = acc[:modes, :] + acc[modes:, :]
    first, second = summed[:, :LANES], summed[:, LANES:]
    rest = acc_low[...]
    low = low_lanes(modes)
    first = first + jnp.where(low, 0.0, rest)
    second = second + jnp.where(low, rest, 0.0)
    first_t, second_t = (first * scale).T, (second * scale).T
    own, to_prev, to_next = first_t[:modes], first_t[modes:], second_t[:modes]
    rows = jnp.concatenate([to_next, own, to_prev], axis=1)
    share = out_ref.shape[1]
    for d in range(out_ref.shape[0]):
        out_ref[d] = rows[d * share:(d + 1) * share]


def contract_blocks(bases, rim, clash, dofs, stiffness, from_left, from_right, pieces, slice_rows, parts, scale):
    total = 2 * sum(p.shape[0] for p in pieces)
    count = rim.size
    modes = LANES // 2
    n_blocks, size = dofs.shape
    wide = lambda n: pltpu.VMEM((n, LANES), F32)
    return pl.pallas_call(
        functools.partial(main_kernel, slice_rows, len(pieces), scale),
        out_shape=jax.ShapeDtypeStruct((parts, modes // parts, 3 * modes), F32),
        in_specs=[SMEM] * 4 + [pl.BlockSpec(memory_space=pltpu.HBM)] + [VMEM] * (2 + len(pieces)),
        out_specs=VMEM,
        scratch_shapes=[
            wide(2 * total + SPARE), wide(count), wide(count), wide(2 * n_blocks * size + SPARE),
            pltpu.VMEM((2 * modes, 2 * LANES), F32), pltpu.VMEM((modes, LANES), F32),
            pltpu.VMEM(stiffness.shape, BF16), pltpu.SemaphoreType.DMA,
        ],
        compiler_params=pltpu.CompilerParams(vmem_limit_bytes=50 * 2**20),
    )(bases, rim, clash, dofs, stiffness, from_left, from_right, *pieces)


def sum_kernel(parts_ref, out_ref):
    total = parts_ref[0]
    for i in range(1, parts_ref.shape[0]):
        total = total + parts_ref[i]
    for i in range(out_ref.shape[0]):
        out_ref[i] = total


def sum_for_all(parts, receivers):
    return pl.pallas_call(
        sum_kernel,
        out_shape=jax.ShapeDtypeStruct((receivers,) + parts.shape[1:], F32),
        in_specs=[VMEM],
        out_specs=VMEM,
        compiler_params=pltpu.CompilerParams(vmem_limit_bytes=8 * 2**20),
    )(parts)


def slots_kernel(me_ref, owner_ref, arrived_ref, out_ref):
    count = arrived_ref.shape[0]
    shape = arrived_ref.shape[1:]
    part = lax.broadcasted_iota(jnp.int32, shape, 1) // (LANES // 2)
    me = me_ref[0]
    filled = jnp.int32(0)
    held = [jnp.int32(-1)] * CAP
    for t in range(count):
        mine = owner_ref[t] == me
        held = [jnp.where(mine & (filled == slot), t, old) for slot, old in enumerate(held)]
        filled = filled + mine.astype(jnp.int32)
    for slot, t in enumerate(held):
        before = jnp.where(t > 0, arrived_ref[jnp.maximum(t - 1, 0)], 0.0)
        after = jnp.where((t >= 0) & (t < count - 1), arrived_ref[jnp.minimum(t + 1, count - 1)], 0.0)
        own = jnp.where(t >= 0, arrived_ref[jnp.maximum(t, 0)], 0.0)
        out_ref[slot] = jnp.where(part == 0, before, jnp.where(part == 1, own, after))


def fill_slots(me, owner_map, arrived):
    return pl.pallas_call(
        slots_kernel,
        out_shape=jax.ShapeDtypeStruct((CAP,) + arrived.shape[1:], F32),
        in_specs=[SMEM, SMEM, VMEM],
        out_specs=VMEM,
        compiler_params=pltpu.CompilerParams(vmem_limit_bytes=8 * 2**20),
    )(me.astype(jnp.int32), owner_map, arrived)


def ring_pieces(packed, index, count, beside):
    ring = count // 2
    move = lambda value, dx, dy: lax.ppermute(
        value, "blk",
        [(i, ((i // ring + dx) % 2) * ring + (i % ring + dy) % ring) for i in range(count)],
    )
    x, y = index // ring, index % ring
    base = lambda flip, dy: ((jnp.remainder(x + flip, 2)) * ring + jnp.remainder(y + dy, ring))
    both = jnp.concatenate([packed, move(packed, 1, 0)], axis=0)
    both, beside = lax.optimization_barrier((both, beside))
    pieces, places = [both], [base(0, 0), base(1, 0)]
    up = down = both
    for k in range(1, ring // 2):
        up, down = move(up, 0, 1), move(down, 0, -1)
        pieces += [up, down]
        places += [base(0, -k), base(1, -k), base(0, k), base(1, k)]
    pieces.append(move(up, 0, 1))
    places += [base(0, -(ring // 2)), base(1, -(ring // 2))]
    return pieces, jnp.stack(places).astype(jnp.int32), beside


def on_device(stiffness, dofmap, eigvecs, rim_rows, owner_map):
    blk_count, sub_count = lax.axis_size("blk"), lax.axis_size("sub")
    own_rows = eigvecs.shape[2]
    slice_rows = own_rows // 2
    block_count, block_size = dofmap.shape[1:]
    blk, sub = lax.axis_index("blk"), lax.axis_index("sub")
    with jax.named_scope("pack"):
        packed = pack(eigvecs[0])
    with jax.named_scope("index_words"):
        dofs, rim, clash = index_words(dofmap[0], lax.optimization_barrier((rim_rows[0], packed))[0])
    with jax.named_scope("gather_modes"):
        pieces, places, (dofs, rim, clash) = ring_pieces(packed, blk, blk_count, (dofs, rim, clash))
        bases = places * own_rows
    with jax.named_scope("rim"):
        left, right = take_rim(bases, rim, pieces, slice_rows)
        from_left = lax.ppermute(right, "sub", [(i, i + 1) for i in range(sub_count - 1)])
        from_right = lax.ppermute(left, "sub", [(i + 1, i) for i in range(sub_count - 1)])
    with jax.named_scope("contract"):
        scale = 1.0 / math.sqrt(block_count * blk_count * block_size)
        share = contract_blocks(
            bases, rim, clash, dofs, stiffness[0], from_left, from_right, pieces, slice_rows, blk_count, scale
        )
    with jax.named_scope("sum_over_blk"):
        sent = sum_for_all(lax.all_to_all(share, "blk", 0, 0, tiled=True), sub_count)
    with jax.named_scope("relay"):
        arrived = lax.all_to_all(sent, "sub", 0, 0, tiled=True)
    with jax.named_scope("slots"):
        return fill_slots(jnp.reshape(sub, (1,)), owner_map, arrived)


def solution(mesh):
    return jax.shard_map(
        on_device,
        mesh=mesh,
        in_specs=(
            P("sub", "blk", None, None),
            P("sub", "blk", None),
            P("sub", None, "blk"),
            P("sub", None, None),
            P(),
        ),
        out_specs=P("sub", "blk", None),
        check_vma=False,
    )
```
